256 devices in a mesh: row: 8 (over x_lo, y), col: 32 (over z, x_hi, core).
Axes of the slice: x: 4 (x_hi: 2, x_lo: 2; x = x_hi * 2 + x_lo), y: 4, z: 8, core: 2. Of those that a mesh axis runs over, the one named last changes fastest.
Arguments:
- features: bfloat16 [2048, 16384], P(None, 'col'), may hold values from -6 to 6
- cross_weight: bfloat16 [16384, 16384], P('row', 'col'), may hold values from -0.046875 to 0.046875
- cross_bias: float32 [16384], P('row'), may hold values from -5 to 5
- expert_ids: int32 [2048, 2], P('col'), may hold values from 0 to 31, all different within a row; in each aligned block of 64 rows (0 to 63, 64 to 127, ...) at most 8 rows name the same one
- route_gates: float32 [2048, 2], P('col'), may hold values from 0.2 to 1
- expert_weight: bfloat16 [32, 16384, 2048], P('col', 'row'), may hold values from -0.046875 to 0.046875
- mixed_grad: bfloat16 [2048, 2048], P('col'), may hold values from -6 to 6
Outputs:
- combined: bfloat16 [2048, 2048], P('col', 'row')
- cross_grad: bfloat16 [2048, 16384], P('col', 'row')
The draws below stay inside these ranges and needn't reach their ends.
Inputs may be any that keep to these rules, and one draw needn't show every extreme that they name: `expert_ids`: each row names two different experts. In each aligned block of 64 rows no expert is named more than 8 times, a bound that some block reaches.
All inputs are finite; a program needn't handle non-finite values.
Results may differ from the reference program's by a relative error of at most 0.025.
Values may be sent and summed in bfloat16 or wider, within the bound.
No kernel may reach another device: no remote copies, remote signals or barrier semaphores. Data moves between devices by JAX's collectives and lax.ppermute only.
A program may use at most 128 MiB of HBM per device.

```python
import math
import jax
import jax.numpy as jnp
import numpy as np
from jax import lax

D = 16384
OUT = 2048
ROWS = 64
BATCH = 2048
EXPERTS = 32
CAP = 8
N_COL = 32


def with_spikes(result, key, source, target, blocks, factor):
    owner, partner = [(jnp.arange(result.shape[axis_at]) // (result.shape[axis_at] // blocks)).reshape([-1 if axis == axis_at else 1 for axis in range(result.ndim)]) for axis_at in (source, target)]
    chosen = jax.random.permutation(key, blocks)[partner]
    strong = (owner == chosen) | (owner == (partner + blocks // 2) % blocks)
    return jnp.where(strong, factor * result, result)


def block_scale(stream_key, extent, cuts, smallest, top_value):
    def one(position, shards_of):
        steps = jax.random.uniform(jax.random.fold_in(jax.random.fold_in(stream_key, 6), position), (shards_of,), jnp.float32, smallest / len(cuts), top_value / len(cuts))
        return jnp.repeat(jnp.exp(steps), extent[position] // shards_of).reshape((-1,) + (1,) * (len(extent) - position - 1))

    loudness = one(*cuts[0])
    for cut in cuts[1:]:
        loudness = loudness * one(*cut)
    return loudness


def deal_out(rng, own, number, rows, number_of, top, bound, slope):
    sequence = jax.random.permutation(rng, number_of)
    heavy_load, usual = shares(number_of, rows * top, bound, slope, True), shares(number_of, rows * top, bound, slope, False)
    places = jnp.arange(number_of)

    def named(sizes, rotation):
        used = int((sizes > 0).sum())
        fixed = max(1, used // 4)
        moved = fixed + (places - fixed + rotation * (used - fixed)) % max(1, number_of - fixed)
        return jnp.zeros((number_of,), jnp.int32).at[sequence[jnp.where(places < fixed, places, moved)]].set(jnp.asarray(sizes, jnp.int32))

    sizes = jnp.where(number % 4 == 0, named(heavy_load, number // 4), named(usual, number - number // 4 - 1))
    mixed = jax.random.permutation(jax.random.fold_in(own, 3), number_of)
    donor, taker = mixed[0:number_of // 2 * 2:2], mixed[1:number_of // 2 * 2:2]
    slack = jnp.minimum(sizes[donor] - 1, bound - sizes[taker]) // 2
    slack = jnp.where((donor == sequence[0]) | (taker == sequence[0]) | (sizes[taker] == 0), 0, jnp.maximum(slack, 0))
    moved = jax.random.randint(jax.random.fold_in(own, 4), (number_of // 2,), 0, 1 << 20) % (slack + 1)
    sizes = sizes.at[donor].add(-moved).at[taker].add(moved)
    members = jnp.searchsorted(jnp.cumsum(sizes), jnp.arange(rows * top), side="right").astype(jnp.int32)
    grid = members.reshape(top, rows).T
    grid = grid[jax.random.permutation(jax.random.fold_in(own, 1), rows)]
    rotation = jax.random.randint(jax.random.fold_in(own, 2), (rows, 1), 0, top)
    return jnp.take_along_axis(grid, (jnp.arange(top)[None, :] + rotation) % top, axis=1)


def shares(number_of, total, most, skew, full):
    portions = [(1 << 20) // math.isqrt(standing ** skew) + 1 for standing in range(1, number_of + 1)]
    largest = most if full else min(most, max(-(-total // number_of), total * portions[0] // sum(portions)))
    least = 1 if total - largest >= number_of - 1 else 0
    holding, surplus = [largest] + [least] * (number_of - 1), total - largest - least * (number_of - 1)
    while surplus > 0:
        movable = [i for i in range(1, number_of) if holding[i] < largest] or [i for i in range(1, number_of) if holding[i] < most]
        whole, budget = sum([portions[i] for i in movable]), surplus
        for i in movable:
            addition = min(most - holding[i], max(1, budget * portions[i] // whole), surplus)
            holding[i] = holding[i] + addition
            surplus = surplus - addition
    return np.array(holding)


def bell_draw(stream_key, extent, spread, most, pieces=(), kind=jnp.bfloat16):
    result = jax.random.normal(stream_key, extent, jnp.float32) * spread
    if len(pieces) > 0:
        result = block_scale(stream_key, extent, pieces, -0.22, 0.18) * result
    return jnp.clip(result, min=-most, max=most).astype(kind)


def noise_with(own_key, extent, deviation, reach, cuts, heavy, kind=jnp.bfloat16):
    entries = deviation * jax.random.normal(own_key, extent, jnp.float32)
    if cuts:
        entries = entries * block_scale(own_key, extent, cuts, -0.22, 0.18)
    return jnp.clip(with_spikes(entries, jax.random.fold_in(own_key, 3), *heavy), -reach, reach).astype(kind)


def setup_inputs(seed: int = 0) -> dict:
    key_list = jax.random.split(jax.random.key(seed), 8)
    features = noise_with(key_list[0], (BATCH, D), 1.0, 6.0, ((1, 32),), (1, 0, 32, 2.75))
    cross_weight = bell_draw(key_list[1], (D, D), D ** -0.5, 0.046875, ((0, 8), (1, 32)))
    cross_bias = bell_draw(key_list[2], (D,), 1.0, 5.0, ((0, 8),), jnp.float32)
    expert_ids_keys = jax.random.split(jax.random.fold_in(key_list[3], 1), BATCH // ROWS)
    expert_ids_turns = jax.random.permutation(jax.random.fold_in(key_list[3], 3), BATCH // ROWS)
    expert_ids = jax.vmap(lambda own, number: deal_out(jax.random.fold_in(key_list[3], 2), own, number, ROWS, EXPERTS, 2, CAP, 2))(expert_ids_keys, expert_ids_turns).reshape((BATCH, 2))
    route_gates = jnp.clip(jnp.exp(math.log(1.0) - 1.609438 * jax.random.uniform(key_list[4], (BATCH, 2), jnp.float32) ** block_scale(key_list[4], (BATCH, 2), ((0, 32),), -0.2, 0.2)), 0.2, 1.0)
    expert_weight = bell_draw(key_list[5], (EXPERTS, D, OUT), D ** -0.5, 0.046875, ((0, 32), (1, 8)))
    mixed_grad = bell_draw(key_list[6], (BATCH, OUT), 1.0, 6.0, ((0, 32),))
    return dict(features=features, cross_weight=cross_weight, cross_bias=cross_bias, expert_ids=expert_ids, route_gates=route_gates, expert_weight=expert_weight, mixed_grad=mixed_grad)


def silu_slope(values):
    sigma = jax.nn.sigmoid(values)
    return sigma * (1.0 + values * (1.0 - sigma))


def reference(features, cross_weight, cross_bias, expert_ids, route_gates, expert_weight, mixed_grad):
    batch_total = features.shape[0]
    width = features.shape[1]
    block_width = width // N_COL
    out_width = expert_weight.shape[2]

    def add_block(index, total):
        start = (index * block_width).astype(jnp.int32)
        left = lax.dynamic_slice_in_dim(features, start, block_width, 1)
        right = lax.dynamic_slice_in_dim(cross_weight, start, block_width, 1)
        term = lax.dot_general(left, right, (((1,), (1,)), ((), ())), preferred_element_type=jnp.float32)
        rounded = lax.optimization_barrier(term.astype(jnp.bfloat16))
        return total + rounded.astype(jnp.float32)

    crossed = lax.fori_loop(0, N_COL, add_block, jnp.zeros((batch_total, width), jnp.float32))
    base_float = features.astype(jnp.float32)
    hidden = (base_float * (crossed + cross_bias) + base_float).astype(jnp.bfloat16)
    route_grad = (route_gates[:, :, None] * mixed_grad[:, None, :].astype(jnp.float32)).astype(jnp.bfloat16)
    flat_ids = expert_ids.reshape(-1)
    pairs = flat_ids.shape[0]
    limit = N_COL * CAP
    flat_grad = route_grad.reshape(pairs, out_width)
    flat_gates = route_gates.reshape(-1)

    def expert_step(index, carry):
        combined_total, grad_total = carry
        chosen = (flat_ids == index).astype(jnp.int32)
        ranking = (jnp.cumsum(chosen) - 1).astype(jnp.int32)
        target = jnp.where(chosen > 0, ranking, limit).astype(jnp.int32)
        slots = jnp.zeros((limit,), jnp.int32).at[target].set(jnp.arange(pairs, dtype=jnp.int32), mode="drop")
        filled = (jnp.arange(limit, dtype=jnp.int32) < jnp.sum(chosen).astype(jnp.int32)).astype(jnp.float32)
        row_of = (slots // 2).astype(jnp.int32)
        weight_now = lax.dynamic_index_in_dim(expert_weight, index, 0, keepdims=False)
        preact = jnp.dot(hidden[row_of], weight_now, preferred_element_type=jnp.float32)
        activated = jax.nn.silu(preact).astype(jnp.bfloat16)
        slope_grad = (flat_grad[slots].astype(jnp.float32) * silu_slope(preact)).astype(jnp.bfloat16)
        back_rows = lax.dot_general(slope_grad, weight_now, (((1,), (1,)), ((), ())), preferred_element_type=jnp.float32).astype(jnp.bfloat16)
        gate_now = flat_gates[slots] * filled
        combined_total = combined_total.at[row_of].add(gate_now[:, None] * activated.astype(jnp.float32))
        grad_total = grad_total.at[row_of].add(filled[:, None] * back_rows.astype(jnp.float32))
        return combined_total, grad_total

    start_state = (jnp.zeros((batch_total, out_width), jnp.float32), jnp.zeros((batch_total, width), jnp.float32))
    combined_total, grad_total = lax.fori_loop(0, N_COL, expert_step, start_state)
    return (combined_total.astype(jnp.bfloat16), grad_total.astype(jnp.bfloat16))
```

```python
import jax
import jax.numpy as jnp
from jax import lax
from jax.sharding import Mesh, PartitionSpec as P

COL = ("z", "xh", "core")
ALL = ("row", "z", "xh", "core")
ROWS_N, Z_N, XH_N, CORE_N = 8, 8, 2, 2
COL_N = Z_N * XH_N * CORE_N
CAP = 8


def swap(values, axis):
    return lax.ppermute(values, axis, [(0, 1), (1, 0)])


def piece(values, index, size, axis=0):
    return lax.dynamic_slice_in_dim(values, index * size, size, axis)


def slot_targets(expert_ids):
    flat = expert_ids.reshape(-1)
    count = flat.shape[0]
    order = jnp.arange(count, dtype=jnp.int32)
    same = (flat[:, None] == flat[None, :]) & (order[None, :] < order[:, None])
    position = jnp.sum(same.astype(jnp.int32), axis=1)
    return flat, position


def local(features, cross_weight, cross_bias, expert_ids, route_gates, expert_weight, mixed_grad):
    row_at = lax.axis_index("row")
    z_at = lax.axis_index("z")
    xh_at = lax.axis_index("xh")
    core_at = lax.axis_index("core")
    batch, block = features.shape
    width = cross_weight.shape[0]
    half = width // 2
    rows = expert_ids.shape[0]
    out_width = expert_weight.shape[2]
    share = out_width // ROWS_N
    slots = COL_N * CAP

    features_there = swap(features, "core")
    weight_there = swap(piece(cross_weight, 1 - core_at, half), "core")
    contract = (((1,), (1,)), ((), ()))
    products = lax.dot_general(
        features, piece(cross_weight, core_at, half), contract, preferred_element_type=jnp.float32
    )
    products = products + lax.dot_general(
        features_there, weight_there, contract, preferred_element_type=jnp.float32
    )
    part = lax.psum_scatter(
        products.astype(jnp.bfloat16), "z", scatter_dimension=0, tiled=True
    )

    perm = []
    for r in range(ROWS_N):
        for z in range(Z_N):
            for u in range(XH_N):
                for v in range(CORE_N):
                    src = ((r * Z_N + z) * XH_N + u) * CORE_N + v
                    dst = ((z * Z_N + r) * XH_N + v) * CORE_N + u
                    perm.append((src, dst))
    plane = lax.ppermute(piece(features, row_at, 4 * rows), ALL, perm)
    base_own = piece(plane, xh_at, 2 * rows)
    base_other = swap(piece(plane, 1 - xh_at, 2 * rows), "xh")
    first = xh_at == 0
    base = jnp.concatenate(
        [jnp.where(first, base_own, base_other), jnp.where(first, base_other, base_own)], axis=1
    ).astype(jnp.float32)

    ids_there = swap(expert_ids, "core")
    flat, position = slot_targets(expert_ids)
    flat_there, position_there = slot_targets(ids_there)
    places = jnp.arange(slots, dtype=jnp.int32)
    target = flat * CAP + position
    table = (places[:, None] == target[None, :]).astype(jnp.bfloat16)
    chooser = jnp.sum(table.reshape(slots, rows, 2), axis=2)
    chip_places = jnp.arange(2 * slots, dtype=jnp.int32)
    here = flat * (2 * CAP) + core_at * CAP + position
    there = flat_there * (2 * CAP) + (1 - core_at) * CAP + position_there
    chip_target = jnp.where(
        core_at == 0, jnp.concatenate([here, there]), jnp.concatenate([there, here])
    )
    chip_chooser = jnp.sum(
        (chip_places[:, None] == chip_target[None, :])
        .astype(jnp.bfloat16)
        .reshape(2 * slots, 2 * rows, 2),
        axis=2,
    )

    grad_share = piece(mixed_grad, row_at, share, 1).astype(jnp.float32)
    route_grad = (route_gates[:, :, None] * grad_share[:, None, :]).astype(jnp.bfloat16)
    send_grad = jnp.dot(
        table, route_grad.reshape(2 * rows, share), preferred_element_type=jnp.float32
    ).astype(jnp.bfloat16)
    routed_grad = lax.all_to_all(
        send_grad.reshape(COL_N, CAP, share), COL, split_axis=0, concat_axis=0, tiled=True
    ).reshape(slots, share)

    part_there = swap(piece(part, 1 - xh_at, 2 * rows), "xh")
    crossed = piece(part, xh_at, 2 * rows).astype(jnp.float32) + part_there.astype(jnp.float32)
    bias = piece(cross_bias, core_at, half)
    hidden = (base * (crossed + bias) + base).astype(jnp.bfloat16)
    send_rows = jnp.dot(chip_chooser, hidden, preferred_element_type=jnp.float32).astype(
        jnp.bfloat16
    )
    routed = lax.all_to_all(
        send_rows.reshape(COL_N, 2 * CAP, half), COL, split_axis=0, concat_axis=0, tiled=True
    ).reshape(COL_N // 2, 2, 2 * CAP, half)

    weight = expert_weight[0]
    pre = jnp.dot(
        routed[:, 0].reshape(slots, half), weight[:half], preferred_element_type=jnp.float32
    ) + jnp.dot(
        routed[:, 1].reshape(slots, half), weight[half:], preferred_element_type=jnp.float32
    )
    pre = pre.astype(jnp.bfloat16).reshape(slots, ROWS_N, share).transpose(1, 0, 2)
    parts = lax.all_to_all(pre, "row", split_axis=0, concat_axis=0, tiled=True)
    preact = jnp.sum(parts.astype(jnp.float32), axis=0)
    sigma = jax.nn.sigmoid(preact)
    activated = (preact * sigma).astype(jnp.bfloat16)
    slope = (
        routed_grad.astype(jnp.float32) * (sigma * (1.0 + preact * (1.0 - sigma)))
    ).astype(jnp.bfloat16)
    slopes = lax.all_to_all(
        jnp.broadcast_to(slope[None], (ROWS_N, slots, share)),
        "row",
        split_axis=0,
        concat_axis=0,
        tiled=True,
    )
    slope_grad = slopes.transpose(1, 0, 2).reshape(slots, out_width)
    back = lax.dot_general(
        slope_grad, weight, contract, preferred_element_type=jnp.float32
    ).astype(jnp.bfloat16)

    answer = jnp.concatenate([back, activated], axis=1).reshape(COL_N, CAP, width + share)
    returned = lax.all_to_all(answer, COL, split_axis=0, concat_axis=0, tiled=True).reshape(
        slots, width + share
    )
    pull = (((0,), (0,)), ((), ()))
    pair_act = lax.dot_general(
        table, returned[:, width:], pull, preferred_element_type=jnp.float32
    )
    combined = jnp.sum(
        route_gates[:, :, None] * pair_act.reshape(rows, 2, share), axis=1
    ).astype(jnp.bfloat16)
    cross_grad = lax.dot_general(
        chooser, returned[:, :width], pull, preferred_element_type=jnp.float32
    ).astype(jnp.bfloat16)
    return combined, cross_grad


def solution(mesh):
    split = Mesh(mesh.devices.reshape(ROWS_N, Z_N, XH_N, CORE_N), ALL)
    return jax.shard_map(
        local,
        mesh=split,
        in_specs=(
            P(None, COL),
            P("row", COL),
            P("row"),
            P(COL, None),
            P(COL, None),
            P(COL, "row", None),
            P(COL, None),
        ),
        out_specs=(P(COL, "row"), P(COL, "row")),
        check_vma=False,
    )
```

```python
import jax
import jax.numpy as jnp
from jax import lax
from jax.sharding import Mesh, PartitionSpec as P

COL = ("z", "xh", "core")
ALL = ("row", "z", "xh", "core")
ROWS_N, Z_N, XH_N, CORE_N = 8, 8, 2, 2
COL_N = Z_N * XH_N * CORE_N
CAP = 8


def swap(values, axis):
    return lax.ppermute(values, axis, [(0, 1), (1, 0)])


def piece(values, index, size, axis=0):
    return lax.dynamic_slice_in_dim(values, index * size, size, axis)


def slot_targets(expert_ids):
    flat = expert_ids.reshape(-1)
    count = flat.shape[0]
    order = jnp.arange(count, dtype=jnp.int32)
    same = (flat[:, None] == flat[None, :]) & (order[None, :] < order[:, None])
    position = jnp.sum(same.astype(jnp.int32), axis=1)
    return flat, position


def local(features, cross_weight, cross_bias, expert_ids, route_gates, expert_weight, mixed_grad):
    row_at = lax.axis_index("row")
    z_at = lax.axis_index("z")
    xh_at = lax.axis_index("xh")
    core_at = lax.axis_index("core")
    batch, block = features.shape
    width = cross_weight.shape[0]
    half = width // 2
    rows = expert_ids.shape[0]
    out_width = expert_weight.shape[2]
    share = out_width // ROWS_N
    slots = COL_N * CAP

    plane_there = (3 * z_at + row_at) % Z_N
    perm = [
        (r * Z_N + z, r * Z_N + (3 * z + r) % Z_N) for r in range(ROWS_N) for z in range(Z_N)
    ]
    plane = lax.ppermute(piece(features, plane_there, 4 * rows), ("row", "z"), perm)

    features_there = swap(features, "core")
    weight_there = swap(piece(cross_weight, 1 - core_at, half), "core")
    contract = (((1,), (1,)), ((), ()))
    products = lax.dot_general(
        features, piece(cross_weight, core_at, half), contract, preferred_element_type=jnp.float32
    )
    products = products + lax.dot_general(
        features_there, weight_there, contract, preferred_element_type=jnp.float32
    )
    products, plane = lax.optimization_barrier((products.astype(jnp.bfloat16), plane))
    part = lax.psum_scatter(products, "z", scatter_dimension=0, tiled=True)

    perm = []
    for r in range(ROWS_N):
        for z in range(Z_N):
            for u in range(XH_N):
                for v in range(CORE_N):
                    src = ((r * Z_N + z) * XH_N + u) * CORE_N + v
                    dst = ((3 * (z - r) % Z_N * Z_N + z) * XH_N + v) * CORE_N + u
                    perm.append((src, dst))
    plane = lax.ppermute(plane, ALL, perm)
    base_own = piece(plane, xh_at, 2 * rows)
    base_other = swap(piece(plane, 1 - xh_at, 2 * rows), "xh")
    first = xh_at == 0
    base = jnp.concatenate(
        [jnp.where(first, base_own, base_other), jnp.where(first, base_other, base_own)], axis=1
    ).astype(jnp.float32)

    ids_there = swap(expert_ids, "core")
    flat, position = slot_targets(expert_ids)
    flat_there, position_there = slot_targets(ids_there)
    places = jnp.arange(slots, dtype=jnp.int32)
    target = flat * CAP + position
    table = (places[:, None] == target[None, :]).astype(jnp.bfloat16)
    chooser = jnp.sum(table.reshape(slots, rows, 2), axis=2)
    chip_places = jnp.arange(2 * slots, dtype=jnp.int32)
    here = flat * (2 * CAP) + core_at * CAP + position
    there = flat_there * (2 * CAP) + (1 - core_at) * CAP + position_there
    chip_target = jnp.where(
        core_at == 0, jnp.concatenate([here, there]), jnp.concatenate([there, here])
    )
    chip_chooser = jnp.sum(
        (chip_places[:, None] == chip_target[None, :])
        .astype(jnp.bfloat16)
        .reshape(2 * slots, 2 * rows, 2),
        axis=2,
    )

    grad_share = piece(mixed_grad, row_at, share, 1).astype(jnp.float32)
    route_grad = (route_gates[:, :, None] * grad_share[:, None, :]).astype(jnp.bfloat16)
    send_grad = jnp.dot(
        table, route_grad.reshape(2 * rows, share), preferred_element_type=jnp.float32
    ).astype(jnp.bfloat16)
    routed_grad = lax.all_to_all(
        send_grad.reshape(COL_N, CAP, share), COL, split_axis=0, concat_axis=0, tiled=True
    ).reshape(slots, share)

    part, base, routed_grad, chip_chooser, chooser, table = lax.optimization_barrier(
        (part, base, routed_grad, chip_chooser, chooser, table)
    )
    part_there = swap(piece(part, 1 - xh_at, 2 * rows), "xh")
    crossed = piece(part, xh_at, 2 * rows).astype(jnp.float32) + part_there.astype(jnp.float32)
    bias = piece(cross_bias, core_at, half)
    hidden = (base * (crossed + bias) + base).astype(jnp.bfloat16)
    send_rows = jnp.dot(chip_chooser, hidden, preferred_element_type=jnp.float32).astype(
        jnp.bfloat16
    )
    routed = lax.all_to_all(
        send_rows.reshape(COL_N, 2 * CAP, half), COL, split_axis=0, concat_axis=0, tiled=True
    ).reshape(COL_N // 2, 2, 2 * CAP, half)

    weight = expert_weight[0]
    pre = jnp.dot(
        routed[:, 0].reshape(slots, half), weight[:half], preferred_element_type=jnp.float32
    ) + jnp.dot(
        routed[:, 1].reshape(slots, half), weight[half:], preferred_element_type=jnp.float32
    )
    pre = pre.astype(jnp.bfloat16).reshape(slots, ROWS_N, share).transpose(1, 0, 2)
    parts = lax.all_to_all(pre, "row", split_axis=0, concat_axis=0, tiled=True)
    preact = jnp.sum(parts.astype(jnp.float32), axis=0)
    sigma = jax.nn.sigmoid(preact)
    activated = (preact * sigma).astype(jnp.bfloat16)
    slope = (
        routed_grad.astype(jnp.float32) * (sigma * (1.0 + preact * (1.0 - sigma)))
    ).astype(jnp.bfloat16)
    slopes = lax.all_to_all(
        jnp.broadcast_to(slope[None], (ROWS_N, slots, share)),
        "row",
        split_axis=0,
        concat_axis=0,
        tiled=True,
    )
    slope_grad = slopes.transpose(1, 0, 2).reshape(slots, out_width)
    back = lax.dot_general(
        slope_grad, weight, contract, preferred_element_type=jnp.float32
    ).astype(jnp.bfloat16)

    answer = jnp.concatenate([back, activated], axis=1).reshape(COL_N, CAP, width + share)
    returned = lax.all_to_all(answer, COL, split_axis=0, concat_axis=0, tiled=True).reshape(
        slots, width + share
    )
    pull = (((0,), (0,)), ((), ()))
    pair_act = lax.dot_general(
        table, returned[:, width:], pull, preferred_element_type=jnp.float32
    )
    combined = jnp.sum(
        route_gates[:, :, None] * pair_act.reshape(rows, 2, share), axis=1
    ).astype(jnp.bfloat16)
    cross_grad = lax.dot_general(
        chooser, returned[:, :width], pull, preferred_element_type=jnp.float32
    ).astype(jnp.bfloat16)
    return combined, cross_grad


def solution(mesh):
    split = Mesh(mesh.devices.reshape(ROWS_N, Z_N, XH_N, CORE_N), ALL)
    return jax.shard_map(
        local,
        mesh=split,
        in_specs=(
            P(None, COL),
            P("row", COL),
            P("row"),
            P(COL, None),
            P(COL, None),
            P(COL, "row", None),
            P(COL, None),
        ),
        out_specs=(P(COL, "row"), P(COL, "row")),
        check_vma=False,
    )
```

```python
import jax
import jax.numpy as jnp
from jax import lax
from jax.experimental import pallas as pl
from jax.experimental.pallas import tpu as pltpu
from jax.sharding import Mesh, PartitionSpec as P

COL = ("z", "xh", "core")
ALL = ("row", "z", "xh", "core")
ROWS_N, Z_N, XH_N, CORE_N = 8, 8, 2, 2
COL_N = Z_N * XH_N * CORE_N
CAP = 8


def swap(values, axis):
    return lax.ppermute(values, axis, [(0, 1), (1, 0)])


def piece(values, index, size, axis=0):
    return lax.dynamic_slice_in_dim(values, index * size, size, axis)


def block_products(at, here, there, weight_here, weight_there):
    contract = (((1,), (1,)), ((), ()))
    own = lax.dot_general(
        here[...], weight_here[...], contract, preferred_element_type=jnp.float32
    )
    other = lax.dot_general(
        there[...], weight_there[...], contract, preferred_element_type=jnp.float32
    )
    return (own + other).astype(jnp.bfloat16)


def early_kernel(at, here, there, weight_here, weight_there, out):
    out[...] = block_products(at, here, there, weight_here, weight_there)


def late_kernel(at, here, there, weight_here, weight_there, own, other):
    values = block_products(at, here, there, weight_here, weight_there)
    rows = values.shape[0] // 2
    low, high = values[:rows], values[rows:]
    first = at[1] == 0

    @pl.when(first)
    def _():
        own[0] = low
        other[0] = high

    @pl.when(jnp.logical_not(first))
    def _():
        own[0] = high
        other[0] = low


def cross_products(part, at, features, features_there, cross_weight, weight_there):
    batch, block = features.shape
    columns = weight_there.shape[0] // 2
    tile = batch // Z_N
    rows = pl.BlockSpec((tile, block), lambda i, at: (i, 0))
    in_specs = [
        rows,
        rows,
        pl.BlockSpec((columns, block), lambda i, at: (2 * at[0] + part, 0)),
        pl.BlockSpec((columns, block), lambda i, at: (part, 0)),
    ]
    if part == 0:
        kernel = early_kernel
        out_specs = pl.BlockSpec((tile, columns), lambda i, at: (i, 0))
        out_shape = jax.ShapeDtypeStruct((batch, columns), jnp.bfloat16)
    else:
        kernel = late_kernel
        out_specs = [pl.BlockSpec((1, tile // 2, columns), lambda i, at: (i, 0, 0))] * 2
        out_shape = [jax.ShapeDtypeStruct((Z_N, tile // 2, columns), jnp.bfloat16)] * 2
    return pl.pallas_call(
        kernel,
        grid_spec=pltpu.PrefetchScalarGridSpec(
            num_scalar_prefetch=1, grid=(Z_N,), in_specs=in_specs, out_specs=out_specs
        ),
        out_shape=out_shape,
        cost_estimate=pl.CostEstimate(
            flops=4 * batch * columns * block, bytes_accessed=7 << 20, transcendentals=0
        ),
    )(at, features, features_there, cross_weight, weight_there)


def slot_targets(expert_ids):
    flat = expert_ids.reshape(-1)
    count = flat.shape[0]
    order = jnp.arange(count, dtype=jnp.int32)
    same = (flat[:, None] == flat[None, :]) & (order[None, :] < order[:, None])
    position = jnp.sum(same.astype(jnp.int32), axis=1)
    return flat, position


def local(features, cross_weight, cross_bias, expert_ids, route_gates, expert_weight, mixed_grad):
    row_at = lax.axis_index("row")
    z_at = lax.axis_index("z")
    xh_at = lax.axis_index("xh")
    core_at = lax.axis_index("core")
    batch, block = features.shape
    width = cross_weight.shape[0]
    half = width // 2
    rows = expert_ids.shape[0]
    out_width = expert_weight.shape[2]
    share = out_width // ROWS_N
    slots = COL_N * CAP

    plane_there = (3 * z_at + row_at) % Z_N
    perm = [
        (r * Z_N + z, r * Z_N + (3 * z + r) % Z_N) for r in range(ROWS_N) for z in range(Z_N)
    ]
    plane = lax.ppermute(piece(features, plane_there, 4 * rows), ("row", "z"), perm)

    features_there = swap(features, "core")
    weight_there = swap(piece(cross_weight, 1 - core_at, half), "core")
    contract = (((1,), (1,)), ((), ()))
    at = jnp.stack([core_at, xh_at]).astype(jnp.int32)
    operands = (at, features, features_there, cross_weight, weight_there)
    part = lax.psum_scatter(
        cross_products(0, *operands), "z", scatter_dimension=0, tiled=True
    )
    late_own, late_other = cross_products(1, *operands)
    late_sum = (
        late_own.astype(jnp.float32) + swap(late_other, "xh").astype(jnp.float32)
    ).astype(jnp.bfloat16)

    perm = []
    for r in range(ROWS_N):
        for z in range(Z_N):
            for u in range(XH_N):
                for v in range(CORE_N):
                    src = ((r * Z_N + z) * XH_N + u) * CORE_N + v
                    dst = ((3 * (z - r) % Z_N * Z_N + z) * XH_N + v) * CORE_N + u
                    perm.append((src, dst))
    plane = lax.ppermute(plane, ALL, perm)
    base_own = piece(plane, xh_at, 2 * rows)
    base_other = swap(piece(plane, 1 - xh_at, 2 * rows), "xh")
    first = xh_at == 0
    base = jnp.concatenate(
        [jnp.where(first, base_own, base_other), jnp.where(first, base_other, base_own)], axis=1
    ).astype(jnp.float32)

    ids_there = swap(expert_ids, "core")
    flat, position = slot_targets(expert_ids)
    flat_there, position_there = slot_targets(ids_there)
    places = jnp.arange(slots, dtype=jnp.int32)
    target = flat * CAP + position
    table = (places[:, None] == target[None, :]).astype(jnp.bfloat16)
    chooser = jnp.sum(table.reshape(slots, rows, 2), axis=2)
    chip_places = jnp.arange(2 * slots, dtype=jnp.int32)
    here = flat * (2 * CAP) + core_at * CAP + position
    there = flat_there * (2 * CAP) + (1 - core_at) * CAP + position_there
    chip_target = jnp.where(
        core_at == 0, jnp.concatenate([here, there]), jnp.concatenate([there, here])
    )
    chip_chooser = jnp.sum(
        (chip_places[:, None] == chip_target[None, :])
        .astype(jnp.bfloat16)
        .reshape(2 * slots, 2 * rows, 2),
        axis=2,
    )

    grad_share = piece(mixed_grad, row_at, share, 1).astype(jnp.float32)
    route_grad = (route_gates[:, :, None] * grad_share[:, None, :]).astype(jnp.bfloat16)
    send_grad = jnp.dot(
        table, route_grad.reshape(2 * rows, share), preferred_element_type=jnp.float32
    ).astype(jnp.bfloat16)
    routed_grad = lax.all_to_all(
        send_grad.reshape(COL_N, CAP, share), COL, split_axis=0, concat_axis=0, tiled=True
    ).reshape(slots, share)

    late_sum, plane, routed_grad = lax.optimization_barrier((late_sum, plane, routed_grad))
    late_parts = lax.all_to_all(late_sum, "z", split_axis=0, concat_axis=0, tiled=True)
    crossed_late = jnp.sum(late_parts.astype(jnp.float32), axis=0)
    part, crossed_late, base, chip_chooser, chooser, table = lax.optimization_barrier(
        (part, crossed_late, base, chip_chooser, chooser, table)
    )
    part_there = swap(piece(part, 1 - xh_at, 2 * rows), "xh")
    crossed_early = piece(part, xh_at, 2 * rows).astype(jnp.float32) + part_there.astype(
        jnp.float32
    )
    crossed = jnp.concatenate([crossed_early, crossed_late], axis=1)
    bias = piece(cross_bias, core_at, half)
    hidden = (base * (crossed + bias) + base).astype(jnp.bfloat16)
    send_rows = jnp.dot(chip_chooser, hidden, preferred_element_type=jnp.float32).astype(
        jnp.bfloat16
    )
    routed = lax.all_to_all(
        send_rows.reshape(COL_N, 2 * CAP, half), COL, split_axis=0, concat_axis=0, tiled=True
    ).reshape(COL_N // 2, 2, 2 * CAP, half)

    weight = expert_weight[0]
    pre = jnp.dot(
        routed[:, 0].reshape(slots, half), weight[:half], preferred_element_type=jnp.float32
    ) + jnp.dot(
        routed[:, 1].reshape(slots, half), weight[half:], preferred_element_type=jnp.float32
    )
    pre = pre.astype(jnp.bfloat16).reshape(slots, ROWS_N, share).transpose(1, 0, 2)
    parts = lax.all_to_all(pre, "row", split_axis=0, concat_axis=0, tiled=True)
    preact = jnp.sum(parts.astype(jnp.float32), axis=0)
    sigma = jax.nn.sigmoid(preact)
    activated = (preact * sigma).astype(jnp.bfloat16)
    slope = (
        routed_grad.astype(jnp.float32) * (sigma * (1.0 + preact * (1.0 - sigma)))
    ).astype(jnp.bfloat16)
    slopes = lax.all_to_all(
        jnp.broadcast_to(slope[None], (ROWS_N, slots, share)),
        "row",
        split_axis=0,
        concat_axis=0,
        tiled=True,
    )
    slope_grad = slopes.transpose(1, 0, 2).reshape(slots, out_width)
    back = lax.dot_general(
        slope_grad, weight, contract, preferred_element_type=jnp.float32
    ).astype(jnp.bfloat16)

    answer = jnp.concatenate([back, activated], axis=1).reshape(COL_N, CAP, width + share)
    returned = lax.all_to_all(answer, COL, split_axis=0, concat_axis=0, tiled=True).reshape(
        slots, width + share
    )
    pull = (((0,), (0,)), ((), ()))
    pair_act = lax.dot_general(
        table, returned[:, width:], pull, preferred_element_type=jnp.float32
    )
    combined = jnp.sum(
        route_gates[:, :, None] * pair_act.reshape(rows, 2, share), axis=1
    ).astype(jnp.bfloat16)
    cross_grad = lax.dot_general(
        chooser, returned[:, :width], pull, preferred_element_type=jnp.float32
    ).astype(jnp.bfloat16)
    return combined, cross_grad


def solution(mesh):
    split = Mesh(mesh.devices.reshape(ROWS_N, Z_N, XH_N, CORE_N), ALL)
    return jax.shard_map(
        local,
        mesh=split,
        in_specs=(
            P(None, COL),
            P("row", COL),
            P("row"),
            P(COL, None),
            P(COL, None),
            P(COL, "row", None),
            P(COL, None),
        ),
        out_specs=(P(COL, "row"), P(COL, "row")),
        check_vma=False,
    )
```

```python
import jax
import jax.numpy as jnp
from jax import lax
from jax.experimental import pallas as pl
from jax.experimental.pallas import tpu as pltpu
from jax.sharding import Mesh, PartitionSpec as P

COL = ("z", "xh", "core")
ALL = ("row", "z", "xh", "core")
ROWS_N, Z_N, XH_N, CORE_N = 8, 8, 2, 2
COL_N = Z_N * XH_N * CORE_N
CAP = 8


def swap(values, axis):
    return lax.ppermute(values, axis, [(0, 1), (1, 0)])


def piece(values, index, size, axis=0):
    return lax.dynamic_slice_in_dim(values, index * size, size, axis)


GRANT = 57 << 20
NT = (((1,), (1,)), ((), ()))


def dot_nt(left, right):
    return lax.dot_general(left, right, NT, preferred_element_type=jnp.float32)


def early_kernel(at, here, there, weight_here, weight_there, out):
    values = dot_nt(here[...], weight_here[...]) + dot_nt(there[...], weight_there[...])
    out[...] = values.astype(jnp.bfloat16)


def late_kernel(at, here, there, weight_here, weight_there, own, other):
    values = dot_nt(here[...], weight_here[...]) + dot_nt(there[...], weight_there[...])
    planes, rows, columns = own.shape
    values = values.astype(jnp.bfloat16).reshape(planes, 2, rows, columns)
    first = at[1] == 0

    @pl.when(first)
    def _():
        own[...] = values[:, 0]
        other[...] = values[:, 1]

    @pl.when(jnp.logical_not(first))
    def _():
        own[...] = values[:, 1]
        other[...] = values[:, 0]


def cross_products(part, at, features, features_there, cross_weight, weight_there):
    batch, block = features.shape
    columns = weight_there.shape[0] // 2
    steps = 2
    tile = batch // steps
    rows = pl.BlockSpec((tile, block), lambda i, at: (i, 0))
    in_specs = [
        rows,
        rows,
        pl.BlockSpec((columns, block), lambda i, at: (2 * at[0] + part, 0)),
        pl.BlockSpec((columns, block), lambda i, at: (part, 0)),
    ]
    if part == 0:
        kernel = early_kernel
        out_specs = pl.BlockSpec((tile, columns), lambda i, at: (i, 0))
        out_shape = jax.ShapeDtypeStruct((batch, columns), jnp.bfloat16)
    else:
        kernel = late_kernel
        planes, half_plane = Z_N // steps, batch // Z_N // 2
        out_specs = [pl.BlockSpec((planes, half_plane, columns), lambda i, at: (i, 0, 0))] * 2
        out_shape = [jax.ShapeDtypeStruct((Z_N, half_plane, columns), jnp.bfloat16)] * 2
    return pl.pallas_call(
        kernel,
        grid_spec=pltpu.PrefetchScalarGridSpec(
            num_scalar_prefetch=1, grid=(steps,), in_specs=in_specs, out_specs=out_specs
        ),
        out_shape=out_shape,
        compiler_params=pltpu.CompilerParams(vmem_limit_bytes=GRANT),
        cost_estimate=pl.CostEstimate(
            flops=4 * batch * columns * block, bytes_accessed=7 << 20, transcendentals=0
        ),
    )(at, features, features_there, cross_weight, weight_there)


def forward_kernel(routed, weight, out):
    shares, slots, share = out.shape
    half = routed.shape[3]
    low = routed[:, 0].reshape(slots, half)
    high = routed[:, 1].reshape(slots, half)
    values = jnp.dot(low, weight[:half], preferred_element_type=jnp.float32)
    values += jnp.dot(high, weight[half:], preferred_element_type=jnp.float32)
    values = values.astype(jnp.bfloat16)
    for index in range(shares):
        out[index] = values[:, index * share : (index + 1) * share]


def expert_forward(routed, weight):
    width, out_width = weight.shape
    share = out_width // ROWS_N
    slots = COL_N * CAP
    shares = 2
    return pl.pallas_call(
        forward_kernel,
        grid=(ROWS_N // shares,),
        in_specs=[
            pl.BlockSpec(routed.shape, lambda i: (0, 0, 0, 0)),
            pl.BlockSpec((width, shares * share), lambda i: (0, i)),
        ],
        out_specs=pl.BlockSpec((shares, slots, share), lambda i: (i, 0, 0)),
        out_shape=jax.ShapeDtypeStruct((ROWS_N, slots, share), jnp.bfloat16),
        compiler_params=pltpu.CompilerParams(vmem_limit_bytes=GRANT),
        cost_estimate=pl.CostEstimate(
            flops=2 * slots * weight.size, bytes_accessed=10 << 20, transcendentals=0
        ),
    )(routed, weight)


def back_kernel(slopes, activated, weight, out):
    shares, slots, share = slopes.shape
    tile = weight.shape[0]
    step = pl.program_id(0)
    values = jnp.zeros((slots, tile), jnp.float32)
    for index in range(shares):
        values += dot_nt(slopes[index], weight[:, index * share : (index + 1) * share])
    out[:, pl.ds(pl.multiple_of(step * tile, tile), tile)] = values.astype(jnp.bfloat16)

    @pl.when(step == 0)
    def _():
        out[:, out.shape[1] - share :] = activated[...]


def expert_back(slopes, activated, weight):
    width, out_width = weight.shape
    slots, share = activated.shape
    steps = 4
    return pl.pallas_call(
        back_kernel,
        grid=(steps,),
        in_specs=[
            pl.BlockSpec(slopes.shape, lambda i: (0, 0, 0)),
            pl.BlockSpec(activated.shape, lambda i: (0, 0)),
            pl.BlockSpec((width // steps, out_width), lambda i: (i, 0)),
        ],
        out_specs=pl.BlockSpec((slots, width + share), lambda i: (0, 0)),
        out_shape=jax.ShapeDtypeStruct((slots, width + share), jnp.bfloat16),
        compiler_params=pltpu.CompilerParams(vmem_limit_bytes=GRANT),
        cost_estimate=pl.CostEstimate(
            flops=2 * slots * weight.size, bytes_accessed=10 << 20, transcendentals=0
        ),
    )(slopes, activated, weight)


def slot_targets(expert_ids):
    flat = expert_ids.reshape(-1)
    count = flat.shape[0]
    order = jnp.arange(count, dtype=jnp.int32)
    same = (flat[:, None] == flat[None, :]) & (order[None, :] < order[:, None])
    position = jnp.sum(same.astype(jnp.int32), axis=1)
    return flat, position


def local(features, cross_weight, cross_bias, expert_ids, route_gates, expert_weight, mixed_grad):
    row_at = lax.axis_index("row")
    z_at = lax.axis_index("z")
    xh_at = lax.axis_index("xh")
    core_at = lax.axis_index("core")
    batch, block = features.shape
    width = cross_weight.shape[0]
    half = width // 2
    rows = expert_ids.shape[0]
    out_width = expert_weight.shape[2]
    share = out_width // ROWS_N
    slots = COL_N * CAP

    plane_there = (3 * z_at + row_at) % Z_N
    perm = [
        (r * Z_N + z, r * Z_N + (3 * z + r) % Z_N) for r in range(ROWS_N) for z in range(Z_N)
    ]
    plane = lax.ppermute(piece(features, plane_there, 4 * rows), ("row", "z"), perm)

    features_there = swap(features, "core")
    weight_there = swap(piece(cross_weight, 1 - core_at, half), "core")
    at = jnp.stack([core_at, xh_at]).astype(jnp.int32)
    operands = (features, features_there, cross_weight, weight_there)
    part = lax.psum_scatter(
        cross_products(0, at, *operands), "z", scatter_dimension=0, tiled=True
    )
    late_own, late_other = cross_products(1, at, *operands)
    late_sum = (
        late_own.astype(jnp.float32) + swap(late_other, "xh").astype(jnp.float32)
    ).astype(jnp.bfloat16)

    perm = []
    for r in range(ROWS_N):
        for z in range(Z_N):
            for u in range(XH_N):
                for v in range(CORE_N):
                    src = ((r * Z_N + z) * XH_N + u) * CORE_N + v
                    dst = ((3 * (z - r) % Z_N * Z_N + z) * XH_N + v) * CORE_N + u
                    perm.append((src, dst))
    plane = lax.ppermute(plane, ALL, perm)
    base_own = piece(plane, xh_at, 2 * rows)
    base_other = swap(piece(plane, 1 - xh_at, 2 * rows), "xh")
    first = xh_at == 0
    base = jnp.concatenate(
        [jnp.where(first, base_own, base_other), jnp.where(first, base_other, base_own)], axis=1
    ).astype(jnp.float32)

    ids_there = swap(expert_ids, "core")
    flat, position = slot_targets(expert_ids)
    flat_there, position_there = slot_targets(ids_there)
    places = jnp.arange(slots, dtype=jnp.int32)
    target = flat * CAP + position
    table = (places[:, None] == target[None, :]).astype(jnp.bfloat16)
    chooser = jnp.sum(table.reshape(slots, rows, 2), axis=2)
    chip_places = jnp.arange(2 * slots, dtype=jnp.int32)
    here = flat * (2 * CAP) + core_at * CAP + position
    there = flat_there * (2 * CAP) + (1 - core_at) * CAP + position_there
    chip_target = jnp.where(
        core_at == 0, jnp.concatenate([here, there]), jnp.concatenate([there, here])
    )
    chip_chooser = jnp.sum(
        (chip_places[:, None] == chip_target[None, :])
        .astype(jnp.bfloat16)
        .reshape(2 * slots, 2 * rows, 2),
        axis=2,
    )

    grad_share = piece(mixed_grad, row_at, share, 1).astype(jnp.float32)
    route_grad = (route_gates[:, :, None] * grad_share[:, None, :]).astype(jnp.bfloat16)
    send_grad = jnp.dot(
        table, route_grad.reshape(2 * rows, share), preferred_element_type=jnp.float32
    ).astype(jnp.bfloat16)
    routed_grad = lax.all_to_all(
        send_grad.reshape(COL_N, CAP, share), COL, split_axis=0, concat_axis=0, tiled=True
    ).reshape(slots, share)

    late_sum, routed_grad = lax.optimization_barrier((late_sum, routed_grad))
    late_parts = lax.all_to_all(late_sum, "z", split_axis=0, concat_axis=0, tiled=True)
    part_there = swap(piece(part, 1 - xh_at, 2 * rows), "xh")
    late_parts, part_there, base, chip_chooser, chooser, table = lax.optimization_barrier(
        (late_parts, part_there, base, chip_chooser, chooser, table)
    )
    crossed_late = jnp.sum(late_parts.astype(jnp.float32), axis=0)
    crossed_early = piece(part, xh_at, 2 * rows).astype(jnp.float32) + part_there.astype(
        jnp.float32
    )
    crossed = jnp.concatenate([crossed_early, crossed_late], axis=1)
    bias = piece(cross_bias, core_at, half)
    hidden = (base * (crossed + bias) + base).astype(jnp.bfloat16)
    send_rows = jnp.dot(chip_chooser, hidden, preferred_element_type=jnp.float32).astype(
        jnp.bfloat16
    )
    routed = lax.all_to_all(
        send_rows.reshape(COL_N, 2 * CAP, half), COL, split_axis=0, concat_axis=0, tiled=True
    ).reshape(COL_N // 2, 2, 2 * CAP, half)

    weight = expert_weight[0]
    pre = expert_forward(routed, weight)
    parts = lax.all_to_all(pre, "row", split_axis=0, concat_axis=0, tiled=True)
    preact = jnp.sum(parts.astype(jnp.float32), axis=0)
    sigma = jax.nn.sigmoid(preact)
    activated = (preact * sigma).astype(jnp.bfloat16)
    slope = (
        routed_grad.astype(jnp.float32) * (sigma * (1.0 + preact * (1.0 - sigma)))
    ).astype(jnp.bfloat16)
    slopes = lax.all_to_all(
        jnp.broadcast_to(slope[None], (ROWS_N, slots, share)),
        "row",
        split_axis=0,
        concat_axis=0,
        tiled=True,
    )
    answer = expert_back(slopes, activated, weight)

    returned = lax.all_to_all(
        answer.reshape(COL_N, CAP, width + share), COL, split_axis=0, concat_axis=0, tiled=True
    ).reshape(slots, width + share)
    pull = (((0,), (0,)), ((), ()))
    pair_act = lax.dot_general(
        table, returned[:, width:], pull, preferred_element_type=jnp.float32
    )
    combined = jnp.sum(
        route_gates[:, :, None] * pair_act.reshape(rows, 2, share), axis=1
    ).astype(jnp.bfloat16)
    cross_grad = lax.dot_general(
        chooser, returned[:, :width], pull, preferred_element_type=jnp.float32
    ).astype(jnp.bfloat16)
    return combined, cross_grad


def solution(mesh):
    split = Mesh(mesh.devices.reshape(ROWS_N, Z_N, XH_N, CORE_N), ALL)
    return jax.shard_map(
        local,
        mesh=split,
        in_specs=(
            P(None, COL),
            P("row", COL),
            P("row"),
            P(COL, None),
            P(COL, None),
            P(COL, "row", None),
            P(COL, None),
        ),
        out_specs=(P(COL, "row"), P(COL, "row")),
        check_vma=False,
    )
```

```python
import jax
import jax.numpy as jnp
from jax import lax
from jax.experimental import pallas as pl
from jax.experimental.pallas import tpu as pltpu
from jax.sharding import Mesh, PartitionSpec as P

COL = ("z", "xh", "core")
ALL = ("row", "z", "xh", "core")
ROWS_N, Z_N, XH_N, CORE_N = 8, 8, 2, 2
COL_N = Z_N * XH_N * CORE_N
CAP = 8


def swap(values, axis):
    return lax.ppermute(values, axis, [(0, 1), (1, 0)])


def piece(values, index, size, axis=0):
    return lax.dynamic_slice_in_dim(values, index * size, size, axis)


EARLY = 640
GRANT = 56 << 20
CHUNKS, CUTS = 4, 4
NT = (((1,), (1,)), ((), ()))
VMEM = pl.BlockSpec(memory_space=pltpu.VMEM)


def dot_nt(left, right):
    return lax.dot_general(left, right, NT, preferred_element_type=jnp.float32)


def products_kernel(at, here, there, weight_here, weight_there, early, own, other):
    values = dot_nt(here[...], weight_here[...]) + dot_nt(there[...], weight_there[...])
    values = values.astype(jnp.bfloat16)
    first_width = early.shape[1]
    planes, rows, columns = own.shape
    early[...] = values[:, :first_width]
    late = values[:, first_width:].reshape(planes, 2, rows, columns)
    first = at[1] == 0

    @pl.when(first)
    def _():
        own[...] = late[:, 0]
        other[...] = late[:, 1]

    @pl.when(jnp.logical_not(first))
    def _():
        own[...] = late[:, 1]
        other[...] = late[:, 0]


def cross_products(at, features, features_there, weight_here, weight_there):
    batch, block = features.shape
    columns = weight_here.shape[0] // 2
    late = columns - EARLY
    steps = 4
    tile = batch // steps
    planes, half_plane = Z_N // steps, batch // Z_N // 2
    rows = pl.BlockSpec((tile, block), lambda i, at: (i, 0))
    weights = pl.BlockSpec((columns, block), lambda i, at: (at[0], 0))
    late_spec = pl.BlockSpec((planes, half_plane, late), lambda i, at: (i, 0, 0))
    late_shape = jax.ShapeDtypeStruct((Z_N, half_plane, late), jnp.bfloat16)
    return pl.pallas_call(
        products_kernel,
        grid_spec=pltpu.PrefetchScalarGridSpec(
            num_scalar_prefetch=1,
            grid=(steps,),
            in_specs=[rows, rows, weights, weights],
            out_specs=[pl.BlockSpec((tile, EARLY), lambda i, at: (i, 0)), late_spec, late_spec],
        ),
        out_shape=[jax.ShapeDtypeStruct((batch, EARLY), jnp.bfloat16), late_shape, late_shape],
        compiler_params=pltpu.CompilerParams(vmem_limit_bytes=GRANT),
        cost_estimate=pl.CostEstimate(
            flops=4 * batch * columns * block, bytes_accessed=10 << 20, transcendentals=0
        ),
    )(at, features, features_there, weight_here, weight_there)


def weight_copies(source, held, semaphores, by_columns):
    rows, columns = source.shape
    copies = []
    for chunk in range(CHUNKS):
        for cut in range(CUTS):
            if by_columns:
                part = (
                    pl.ds(cut * (rows // CUTS), rows // CUTS),
                    pl.ds(chunk * (columns // CHUNKS), columns // CHUNKS),
                )
            else:
                part = (pl.ds((chunk * CUTS + cut) * (rows // CHUNKS // CUTS), rows // CHUNKS // CUTS),)
            copies.append(
                pltpu.make_async_copy(
                    source.at[part], held.at[part], semaphores.at[chunk * CUTS + cut]
                )
            )
    return copies


def forward_kernel(routed, weight, out, held, semaphores):
    copies = weight_copies(weight, held, semaphores, True)
    for copy in copies:
        copy.start()
    shares, slots, share = out.shape
    half = routed.shape[3]
    wide = held.shape[1] // CHUNKS
    low = routed[:, 0].reshape(slots, half)
    high = routed[:, 1].reshape(slots, half)
    for chunk in range(CHUNKS):
        for copy in copies[chunk * CUTS : (chunk + 1) * CUTS]:
            copy.wait()
        columns = slice(chunk * wide, (chunk + 1) * wide)
        values = jnp.dot(low, held[:half, columns], preferred_element_type=jnp.float32)
        values += jnp.dot(high, held[half:, columns], preferred_element_type=jnp.float32)
        values = values.astype(jnp.bfloat16)
        for index in range(wide // share):
            out[chunk * (wide // share) + index] = values[:, index * share : (index + 1) * share]


def back_kernel(slopes, activated, weight, out, held, semaphores):
    copies = weight_copies(weight, held, semaphores, False)
    for copy in copies:
        copy.start()
    shares, slots, share = slopes.shape
    width = held.shape[0]
    tall = width // CHUNKS
    out[:, width:] = activated[...]
    for chunk in range(CHUNKS):
        for copy in copies[chunk * CUTS : (chunk + 1) * CUTS]:
            copy.wait()
        rows = slice(chunk * tall, (chunk + 1) * tall)
        values = jnp.zeros((slots, tall), jnp.float32)
        for index in range(shares):
            values += dot_nt(slopes[index], held[rows, index * share : (index + 1) * share])
        out[:, rows] = values.astype(jnp.bfloat16)


def expert_call(kernel, out_shape, *operands):
    weight = operands[-1]
    return pl.pallas_call(
        kernel,
        in_specs=[VMEM] * (len(operands) - 1) + [pl.BlockSpec(memory_space=pl.ANY)],
        out_specs=VMEM,
        out_shape=jax.ShapeDtypeStruct(out_shape, jnp.bfloat16),
        scratch_shapes=[
            pltpu.VMEM(weight.shape, weight.dtype),
            pltpu.SemaphoreType.DMA((CHUNKS * CUTS,)),
        ],
        compiler_params=pltpu.CompilerParams(vmem_limit_bytes=GRANT),
        cost_estimate=pl.CostEstimate(
            flops=2 * COL_N * CAP * weight.size, bytes_accessed=10 << 20, transcendentals=0
        ),
    )(*operands)


def slot_targets(expert_ids):
    flat = expert_ids.reshape(-1)
    count = flat.shape[0]
    order = jnp.arange(count, dtype=jnp.int32)
    same = (flat[:, None] == flat[None, :]) & (order[None, :] < order[:, None])
    position = jnp.sum(same.astype(jnp.int32), axis=1)
    return flat, position


def local(features, cross_weight, cross_bias, expert_ids, route_gates, expert_weight, mixed_grad):
    row_at = lax.axis_index("row")
    z_at = lax.axis_index("z")
    xh_at = lax.axis_index("xh")
    core_at = lax.axis_index("core")
    batch, block = features.shape
    width = cross_weight.shape[0]
    half = width // 2
    rows = expert_ids.shape[0]
    out_width = expert_weight.shape[2]
    share = out_width // ROWS_N
    slots = COL_N * CAP

    plane_there = (3 * z_at + row_at) % Z_N
    perm = [
        (r * Z_N + z, r * Z_N + (3 * z + r) % Z_N) for r in range(ROWS_N) for z in range(Z_N)
    ]
    plane = lax.ppermute(piece(features, plane_there, 4 * rows), ("row", "z"), perm)

    features_there = swap(features, "core")
    weight_there = swap(cross_weight, "core")
    at = jnp.stack([core_at, xh_at]).astype(jnp.int32)
    early, late_own, late_other = cross_products(
        at, features, features_there, cross_weight, weight_there
    )
    part = lax.psum_scatter(early, "z", scatter_dimension=0, tiled=True)
    late_sum = (
        late_own.astype(jnp.float32) + swap(late_other, "xh").astype(jnp.float32)
    ).astype(jnp.bfloat16)

    perm = []
    for r in range(ROWS_N):
        for z in range(Z_N):
            for u in range(XH_N):
                for v in range(CORE_N):
                    src = ((r * Z_N + z) * XH_N + u) * CORE_N + v
                    dst = ((3 * (z - r) % Z_N * Z_N + z) * XH_N + v) * CORE_N + u
                    perm.append((src, dst))
    plane = lax.ppermute(plane, ALL, perm)
    base_own = piece(plane, xh_at, 2 * rows)
    base_other = swap(piece(plane, 1 - xh_at, 2 * rows), "xh")
    first = xh_at == 0
    base = jnp.concatenate(
        [jnp.where(first, base_own, base_other), jnp.where(first, base_other, base_own)], axis=1
    ).astype(jnp.float32)

    ids_there = swap(expert_ids, "core")
    flat, position = slot_targets(expert_ids)
    flat_there, position_there = slot_targets(ids_there)
    places = jnp.arange(slots, dtype=jnp.int32)
    target = flat * CAP + position
    table = (places[:, None] == target[None, :]).astype(jnp.bfloat16)
    chooser = jnp.sum(table.reshape(slots, rows, 2), axis=2)
    chip_places = jnp.arange(2 * slots, dtype=jnp.int32)
    here = flat * (2 * CAP) + core_at * CAP + position
    there = flat_there * (2 * CAP) + (1 - core_at) * CAP + position_there
    chip_target = jnp.where(
        core_at == 0, jnp.concatenate([here, there]), jnp.concatenate([there, here])
    )
    chip_chooser = jnp.sum(
        (chip_places[:, None] == chip_target[None, :])
        .astype(jnp.bfloat16)
        .reshape(2 * slots, 2 * rows, 2),
        axis=2,
    )

    grad_share = piece(mixed_grad, row_at, share, 1).astype(jnp.float32)
    route_grad = (route_gates[:, :, None] * grad_share[:, None, :]).astype(jnp.bfloat16)
    send_grad = jnp.dot(
        table, route_grad.reshape(2 * rows, share), preferred_element_type=jnp.float32
    ).astype(jnp.bfloat16)

    late_parts = lax.all_to_all(late_sum, "z", split_axis=0, concat_axis=0, tiled=True)
    send_grad, late_parts = lax.optimization_barrier((send_grad, late_parts))
    routed_grad = lax.all_to_all(
        send_grad.reshape(COL_N, CAP, share), COL, split_axis=0, concat_axis=0, tiled=True
    ).reshape(slots, share)
    part_there = swap(piece(part, 1 - xh_at, 2 * rows), "xh")
    part_there, routed_grad, base, chip_chooser, chooser, table = lax.optimization_barrier(
        (part_there, routed_grad, base, chip_chooser, chooser, table)
    )
    crossed_late = jnp.sum(late_parts.astype(jnp.float32), axis=0)
    crossed_early = piece(part, xh_at, 2 * rows).astype(jnp.float32) + part_there.astype(
        jnp.float32
    )
    crossed = jnp.concatenate([crossed_early, crossed_late], axis=1)
    bias = piece(cross_bias, core_at, half)
    hidden = (base * (crossed + bias) + base).astype(jnp.bfloat16)
    send_rows = jnp.dot(chip_chooser, hidden, preferred_element_type=jnp.float32).astype(
        jnp.bfloat16
    )
    routed = lax.all_to_all(
        send_rows.reshape(COL_N, 2 * CAP, half), COL, split_axis=0, concat_axis=0, tiled=True
    ).reshape(COL_N // 2, 2, 2 * CAP, half)

    weight = expert_weight[0]
    pre = expert_call(forward_kernel, (ROWS_N, slots, share), routed, weight)
    parts = lax.all_to_all(pre, "row", split_axis=0, concat_axis=0, tiled=True)
    preact = jnp.sum(parts.astype(jnp.float32), axis=0)
    sigma = jax.nn.sigmoid(preact)
    activated = (preact * sigma).astype(jnp.bfloat16)
    slope = (
        routed_grad.astype(jnp.float32) * (sigma * (1.0 + preact * (1.0 - sigma)))
    ).astype(jnp.bfloat16)
    slopes = lax.all_to_all(
        jnp.broadcast_to(slope[None], (ROWS_N, slots, share)),
        "row",
        split_axis=0,
        concat_axis=0,
        tiled=True,
    )
    answer = expert_call(back_kernel, (slots, width + share), slopes, activated, weight)

    returned = lax.all_to_all(
        answer.reshape(COL_N, CAP, width + share), COL, split_axis=0, concat_axis=0, tiled=True
    ).reshape(slots, width + share)
    pull = (((0,), (0,)), ((), ()))
    pair_act = lax.dot_general(
        table, returned[:, width:], pull, preferred_element_type=jnp.float32
    )
    combined = jnp.sum(
        route_gates[:, :, None] * pair_act.reshape(rows, 2, share), axis=1
    ).astype(jnp.bfloat16)
    cross_grad = lax.dot_general(
        chooser, returned[:, :width], pull, preferred_element_type=jnp.float32
    ).astype(jnp.bfloat16)
    return combined, cross_grad


def solution(mesh):
    split = Mesh(mesh.devices.reshape(ROWS_N, Z_N, XH_N, CORE_N), ALL)
    return jax.shard_map(
        local,
        mesh=split,
        in_specs=(
            P(None, COL),
            P("row", COL),
            P("row"),
            P(COL, None),
            P(COL, None),
            P(COL, "row", None),
            P(COL, None),
        ),
        out_specs=(P(COL, "row"), P(COL, "row")),
        check_vma=False,
    )
```

```python
import jax
import jax.numpy as jnp
from jax import lax
from jax.experimental import pallas as pl
from jax.experimental.pallas import tpu as pltpu
from jax.sharding import Mesh, PartitionSpec as P

COL = ("z", "xh", "core")
ALL = ("row", "z", "xh", "core")
ROWS_N, Z_N, XH_N, CORE_N = 8, 8, 2, 2
COL_N = Z_N * XH_N * CORE_N
CAP = 8


def swap(values, axis):
    return lax.ppermute(values, axis, [(0, 1), (1, 0)])


def piece(values, index, size, axis=0):
    return lax.dynamic_slice_in_dim(values, index * size, size, axis)


EARLY = 512
GRANT = 56 << 20
CHUNKS, CUTS = 4, 4
NT = (((1,), (1,)), ((), ()))
VMEM = pl.BlockSpec(memory_space=pltpu.VMEM)


def dot_nt(left, right):
    return lax.dot_general(left, right, NT, preferred_element_type=jnp.float32)


def products_kernel(at, here, there, weight_here, weight_there, early, own, other):
    values = dot_nt(here[...], weight_here[...]) + dot_nt(there[...], weight_there[...])
    values = values.astype(jnp.bfloat16)
    first_width = early.shape[1]
    planes, rows, columns = own.shape
    early[...] = values[:, :first_width]
    late = values[:, first_width:].reshape(planes, 2, rows, columns)
    first = at[1] == 0

    @pl.when(first)
    def _():
        own[...] = late[:, 0]
        other[...] = late[:, 1]

    @pl.when(jnp.logical_not(first))
    def _():
        own[...] = late[:, 1]
        other[...] = late[:, 0]


def cross_products(at, features, features_there, weight_here, weight_there):
    batch, block = features.shape
    columns = weight_here.shape[0] // 2
    late = columns - EARLY
    steps = 4
    tile = batch // steps
    planes, half_plane = Z_N // steps, batch // Z_N // 2
    rows = pl.BlockSpec((tile, block), lambda i, at: (i, 0))
    weights = pl.BlockSpec((columns, block), lambda i, at: (at[0], 0))
    late_spec = pl.BlockSpec((planes, half_plane, late), lambda i, at: (i, 0, 0))
    late_shape = jax.ShapeDtypeStruct((Z_N, half_plane, late), jnp.bfloat16)
    return pl.pallas_call(
        products_kernel,
        grid_spec=pltpu.PrefetchScalarGridSpec(
            num_scalar_prefetch=1,
            grid=(steps,),
            in_specs=[rows, rows, weights, weights],
            out_specs=[pl.BlockSpec((tile, EARLY), lambda i, at: (i, 0)), late_spec, late_spec],
        ),
        out_shape=[jax.ShapeDtypeStruct((batch, EARLY), jnp.bfloat16), late_shape, late_shape],
        compiler_params=pltpu.CompilerParams(vmem_limit_bytes=GRANT),
        cost_estimate=pl.CostEstimate(
            flops=4 * batch * columns * block, bytes_accessed=10 << 20, transcendentals=0
        ),
    )(at, features, features_there, weight_here, weight_there)


def weight_copies(source, held, semaphores, by_columns):
    rows, columns = source.shape
    copies = []
    for chunk in range(CHUNKS):
        for cut in range(CUTS):
            if by_columns:
                part = (
                    pl.ds(cut * (rows // CUTS), rows // CUTS),
                    pl.ds(chunk * (columns // CHUNKS), columns // CHUNKS),
                )
            else:
                part = (pl.ds((chunk * CUTS + cut) * (rows // CHUNKS // CUTS), rows // CHUNKS // CUTS),)
            copies.append(
                pltpu.make_async_copy(
                    source.at[part], held.at[part], semaphores.at[chunk * CUTS + cut]
                )
            )
    return copies


def forward_kernel(routed, weight, out, held, semaphores):
    copies = weight_copies(weight, held, semaphores, True)
    for copy in copies:
        copy.start()
    shares, slots, share = out.shape
    half = held.shape[0] // 2
    wide = held.shape[1] // CHUNKS
    low = routed[:, 0, :, :half].reshape(slots, half)
    high = routed[:, 1, :, :half].reshape(slots, half)
    for chunk in range(CHUNKS):
        for copy in copies[chunk * CUTS : (chunk + 1) * CUTS]:
            copy.wait()
        columns = slice(chunk * wide, (chunk + 1) * wide)
        values = jnp.dot(low, held[:half, columns], preferred_element_type=jnp.float32)
        values += jnp.dot(high, held[half:, columns], preferred_element_type=jnp.float32)
        values = values.astype(jnp.bfloat16)
        for index in range(wide // share):
            out[chunk * (wide // share) + index] = values[:, index * share : (index + 1) * share]


def back_kernel(slopes, activated, weight, out, held, semaphores):
    copies = weight_copies(weight, held, semaphores, False)
    for copy in copies:
        copy.start()
    shares, slots, share = slopes.shape
    width = held.shape[0]
    tall = width // CHUNKS
    out[:, width:] = activated[...]
    for chunk in range(CHUNKS):
        for copy in copies[chunk * CUTS : (chunk + 1) * CUTS]:
            copy.wait()
        rows = slice(chunk * tall, (chunk + 1) * tall)
        values = jnp.zeros((slots, tall), jnp.float32)
        for index in range(shares):
            values += dot_nt(slopes[index], held[rows, index * share : (index + 1) * share])
        out[:, rows] = values.astype(jnp.bfloat16)


def expert_call(kernel, out_shape, *operands):
    weight = operands[-1]
    return pl.pallas_call(
        kernel,
        in_specs=[VMEM] * (len(operands) - 1) + [pl.BlockSpec(memory_space=pl.ANY)],
        out_specs=VMEM,
        out_shape=jax.ShapeDtypeStruct(out_shape, jnp.bfloat16),
        scratch_shapes=[
            pltpu.VMEM(weight.shape, weight.dtype),
            pltpu.SemaphoreType.DMA((CHUNKS * CUTS,)),
        ],
        compiler_params=pltpu.CompilerParams(vmem_limit_bytes=GRANT),
        cost_estimate=pl.CostEstimate(
            flops=2 * COL_N * CAP * weight.size, bytes_accessed=10 << 20, transcendentals=0
        ),
    )(*operands)


def slot_targets(expert_ids):
    flat = expert_ids.reshape(-1)
    count = flat.shape[0]
    order = jnp.arange(count, dtype=jnp.int32)
    same = (flat[:, None] == flat[None, :]) & (order[None, :] < order[:, None])
    position = jnp.sum(same.astype(jnp.int32), axis=1)
    return flat, position


def local(features, cross_weight, cross_bias, expert_ids, route_gates, expert_weight, mixed_grad):
    row_at = lax.axis_index("row")
    z_at = lax.axis_index("z")
    xh_at = lax.axis_index("xh")
    core_at = lax.axis_index("core")
    batch, block = features.shape
    width = cross_weight.shape[0]
    half = width // 2
    rows = expert_ids.shape[0]
    out_width = expert_weight.shape[2]
    share = out_width // ROWS_N
    slots = COL_N * CAP

    features_there = swap(features, "core")
    weight_there = swap(cross_weight, "core")
    at = jnp.stack([core_at, xh_at]).astype(jnp.int32)
    early, late_own, late_other = cross_products(
        at, features, features_there, cross_weight, weight_there
    )
    part = lax.psum_scatter(early, "z", scatter_dimension=0, tiled=True)
    late_sum = (
        late_own.astype(jnp.float32) + swap(late_other, "xh").astype(jnp.float32)
    ).astype(jnp.bfloat16)

    held_features, late_sum = lax.optimization_barrier((features, late_sum))
    plane_there = (3 * z_at + row_at) % Z_N
    pieces = []
    for turn in range(2):
        perm = []
        for r in range(ROWS_N):
            for z in range(Z_N):
                for u in range(XH_N):
                    for v in range(CORE_N):
                        src = ((r * Z_N + z) * XH_N + u) * CORE_N + v
                        dst = ((z * Z_N + (3 * z + r) % Z_N) * XH_N + (v ^ turn)) * CORE_N + u
                        perm.append((src, dst))
        chip_there = plane_there * XH_N + (core_at ^ turn)
        pieces.append(lax.ppermute(piece(held_features, chip_there, 2 * rows), ALL, perm))
    first = xh_at == 0
    base = jnp.concatenate(
        [jnp.where(first, pieces[0], pieces[1]), jnp.where(first, pieces[1], pieces[0])], axis=1
    ).astype(jnp.float32)

    ids_there = swap(expert_ids, "core")
    flat, position = slot_targets(expert_ids)
    flat_there, position_there = slot_targets(ids_there)
    places = jnp.arange(slots, dtype=jnp.int32)
    target = flat * CAP + position
    table = (places[:, None] == target[None, :]).astype(jnp.bfloat16)
    chooser = jnp.sum(table.reshape(slots, rows, 2), axis=2)
    chip_places = jnp.arange(2 * slots, dtype=jnp.int32)
    here = flat * (2 * CAP) + core_at * CAP + position
    there = flat_there * (2 * CAP) + (1 - core_at) * CAP + position_there
    chip_target = jnp.where(
        core_at == 0, jnp.concatenate([here, there]), jnp.concatenate([there, here])
    )
    chip_chooser = jnp.sum(
        (chip_places[:, None] == chip_target[None, :])
        .astype(jnp.bfloat16)
        .reshape(2 * slots, 2 * rows, 2),
        axis=2,
    )

    grad_share = piece(mixed_grad, row_at, share, 1).astype(jnp.float32)
    route_grad = (route_gates[:, :, None] * grad_share[:, None, :]).astype(jnp.bfloat16)
    send_grad = jnp.dot(
        table, route_grad.reshape(2 * rows, share), preferred_element_type=jnp.float32
    ).astype(jnp.bfloat16)
    lanes = share // 2
    send_grad = send_grad.reshape(COL_N, CAP, share)
    send_grad = jnp.concatenate([send_grad[:, :, :lanes], send_grad[:, :, lanes:]], axis=1)

    late_parts = lax.all_to_all(late_sum, "z", split_axis=0, concat_axis=0, tiled=True)
    part_there = swap(piece(part, 1 - xh_at, 2 * rows), "xh")
    late_parts, part_there, base, chip_chooser, chooser, table, send_grad = (
        lax.optimization_barrier(
            (late_parts, part_there, base, chip_chooser, chooser, table, send_grad)
        )
    )
    crossed_late = jnp.sum(late_parts.astype(jnp.float32), axis=0)
    crossed_early = piece(part, xh_at, 2 * rows).astype(jnp.float32) + part_there.astype(
        jnp.float32
    )
    crossed = jnp.concatenate([crossed_early, crossed_late], axis=1)
    bias = piece(cross_bias, core_at, half)
    hidden = (base * (crossed + bias) + base).astype(jnp.bfloat16)
    send_rows = jnp.dot(chip_chooser, hidden, preferred_element_type=jnp.float32).astype(
        jnp.bfloat16
    )
    send = jnp.concatenate([send_rows.reshape(COL_N, 2 * CAP, half), send_grad], axis=2)
    routed = lax.all_to_all(send, COL, split_axis=0, concat_axis=0, tiled=True)
    grad = routed[:, :, half:]
    routed_grad = jnp.concatenate([grad[:, :CAP], grad[:, CAP:]], axis=2).reshape(slots, share)
    routed = routed.reshape(COL_N // 2, 2, 2 * CAP, half + lanes)

    weight = expert_weight[0]
    pre = expert_call(forward_kernel, (ROWS_N, slots, share), routed, weight)
    parts = lax.all_to_all(pre, "row", split_axis=0, concat_axis=0, tiled=True)
    preact = jnp.sum(parts.astype(jnp.float32), axis=0)
    sigma = jax.nn.sigmoid(preact)
    activated = (preact * sigma).astype(jnp.bfloat16)
    slope = (
        routed_grad.astype(jnp.float32) * (sigma * (1.0 + preact * (1.0 - sigma)))
    ).astype(jnp.bfloat16)
    slopes = lax.all_to_all(
        jnp.broadcast_to(slope[None], (ROWS_N, slots, share)),
        "row",
        split_axis=0,
        concat_axis=0,
        tiled=True,
    )
    answer = expert_call(back_kernel, (slots, width + share), slopes, activated, weight)

    returned = lax.all_to_all(
        answer.reshape(COL_N, CAP, width + share), COL, split_axis=0, concat_axis=0, tiled=True
    ).reshape(slots, width + share)
    pull = (((0,), (0,)), ((), ()))
    pair_act = lax.dot_general(
        table, returned[:, width:], pull, preferred_element_type=jnp.float32
    )
    combined = jnp.sum(
        route_gates[:, :, None] * pair_act.reshape(rows, 2, share), axis=1
    ).astype(jnp.bfloat16)
    cross_grad = lax.dot_general(
        chooser, returned[:, :width], pull, preferred_element_type=jnp.float32
    ).astype(jnp.bfloat16)
    return combined, cross_grad


def solution(mesh):
    split = Mesh(mesh.devices.reshape(ROWS_N, Z_N, XH_N, CORE_N), ALL)
    return jax.shard_map(
        local,
        mesh=split,
        in_specs=(
            P(None, COL),
            P("row", COL),
            P("row"),
            P(COL, None),
            P(COL, None),
            P(COL, "row", None),
            P(COL, None),
        ),
        out_specs=(P(COL, "row"), P(COL, "row")),
        check_vma=False,
    )
```

```python
import jax
import jax.numpy as jnp
from jax import lax
from jax.experimental import pallas as pl
from jax.experimental.pallas import tpu as pltpu
from jax.sharding import Mesh, PartitionSpec as P

COL = ("z", "xh", "core")
ALL = ("row", "z", "xh", "core")
ROWS_N, Z_N, XH_N, CORE_N = 8, 8, 2, 2
COL_N = Z_N * XH_N * CORE_N
CAP = 8


def swap(values, axis):
    return lax.ppermute(values, axis, [(0, 1), (1, 0)])


def piece(values, index, size, axis=0):
    return lax.dynamic_slice_in_dim(values, index * size, size, axis)


EARLY = 512
GRANT = 56 << 20
CHUNKS, CUTS = 4, 4
NT = (((1,), (1,)), ((), ()))
VMEM = pl.BlockSpec(memory_space=pltpu.VMEM)


def dot_nt(left, right):
    return lax.dot_general(left, right, NT, preferred_element_type=jnp.float32)


def products_kernel(at, here, there, weight_here, weight_there, early, own, other):
    values = dot_nt(here[...], weight_here[...]) + dot_nt(there[...], weight_there[...])
    values = values.astype(jnp.bfloat16)
    first_width = early.shape[1]
    planes, rows, columns = own.shape
    early[...] = values[:, :first_width]
    late = values[:, first_width:].reshape(planes, 2, rows, columns)
    first = at[1] == 0

    @pl.when(first)
    def _():
        own[...] = late[:, 0]
        other[...] = late[:, 1]

    @pl.when(jnp.logical_not(first))
    def _():
        own[...] = late[:, 1]
        other[...] = late[:, 0]


def cross_products(at, features, features_there, weight_here, weight_there):
    batch, block = features.shape
    columns = weight_here.shape[0] // 2
    late = columns - EARLY
    steps = 4
    tile = batch // steps
    planes, half_plane = Z_N // steps, batch // Z_N // 2
    rows = pl.BlockSpec((tile, block), lambda i, at: (i, 0))
    weights = pl.BlockSpec((columns, block), lambda i, at: (at[0], 0))
    late_spec = pl.BlockSpec((planes, half_plane, late), lambda i, at: (i, 0, 0))
    late_shape = jax.ShapeDtypeStruct((Z_N, half_plane, late), jnp.bfloat16)
    return pl.pallas_call(
        products_kernel,
        grid_spec=pltpu.PrefetchScalarGridSpec(
            num_scalar_prefetch=1,
            grid=(steps,),
            in_specs=[rows, rows, weights, weights],
            out_specs=[pl.BlockSpec((tile, EARLY), lambda i, at: (i, 0)), late_spec, late_spec],
        ),
        out_shape=[jax.ShapeDtypeStruct((batch, EARLY), jnp.bfloat16), late_shape, late_shape],
        compiler_params=pltpu.CompilerParams(vmem_limit_bytes=GRANT),
        cost_estimate=pl.CostEstimate(
            flops=4 * batch * columns * block, bytes_accessed=10 << 20, transcendentals=0
        ),
    )(at, features, features_there, weight_here, weight_there)


def weight_copies(source, held, semaphores, by_columns):
    rows, columns = source.shape
    copies = []
    for chunk in range(CHUNKS):
        for cut in range(CUTS):
            if by_columns:
                part = (
                    pl.ds(cut * (rows // CUTS), rows // CUTS),
                    pl.ds(chunk * (columns // CHUNKS), columns // CHUNKS),
                )
            else:
                part = (pl.ds((chunk * CUTS + cut) * (rows // CHUNKS // CUTS), rows // CHUNKS // CUTS),)
            copies.append(
                pltpu.make_async_copy(
                    source.at[part], held.at[part], semaphores.at[chunk * CUTS + cut]
                )
            )
    return copies


def forward_kernel(routed, weight, out, held, semaphores):
    copies = weight_copies(weight, held, semaphores, True)
    for copy in copies:
        copy.start()
    shares, slots, share = out.shape
    half = held.shape[0] // 2
    wide = held.shape[1] // CHUNKS
    low = routed[:, 0, :, :half].reshape(slots, half)
    high = routed[:, 1, :, :half].reshape(slots, half)
    for chunk in range(CHUNKS):
        for copy in copies[chunk * CUTS : (chunk + 1) * CUTS]:
            copy.wait()
        columns = slice(chunk * wide, (chunk + 1) * wide)
        values = jnp.dot(low, held[:half, columns], preferred_element_type=jnp.float32)
        values += jnp.dot(high, held[half:, columns], preferred_element_type=jnp.float32)
        values = values.astype(jnp.bfloat16)
        for index in range(wide // share):
            out[chunk * (wide // share) + index] = values[:, index * share : (index + 1) * share]


def back_kernel(slopes, activated, weight, out, held, semaphores):
    copies = weight_copies(weight, held, semaphores, False)
    for copy in copies:
        copy.start()
    shares, slots, share = slopes.shape
    width = held.shape[0]
    tall = width // CHUNKS
    out[:, width:] = activated[...]
    for chunk in range(CHUNKS):
        for copy in copies[chunk * CUTS : (chunk + 1) * CUTS]:
            copy.wait()
        rows = slice(chunk * tall, (chunk + 1) * tall)
        values = jnp.zeros((slots, tall), jnp.float32)
        for index in range(shares):
            values += dot_nt(slopes[index], held[rows, index * share : (index + 1) * share])
        out[:, rows] = values.astype(jnp.bfloat16)


def expert_call(kernel, out_shape, *operands):
    weight = operands[-1]
    return pl.pallas_call(
        kernel,
        in_specs=[VMEM] * (len(operands) - 1) + [pl.BlockSpec(memory_space=pl.ANY)],
        out_specs=VMEM,
        out_shape=jax.ShapeDtypeStruct(out_shape, jnp.bfloat16),
        scratch_shapes=[
            pltpu.VMEM(weight.shape, weight.dtype),
            pltpu.SemaphoreType.DMA((CHUNKS * CUTS,)),
        ],
        compiler_params=pltpu.CompilerParams(vmem_limit_bytes=GRANT),
        cost_estimate=pl.CostEstimate(
            flops=2 * COL_N * CAP * weight.size, bytes_accessed=10 << 20, transcendentals=0
        ),
    )(*operands)


def slot_targets(expert_ids):
    flat = expert_ids.reshape(-1)
    count = flat.shape[0]
    order = jnp.arange(count, dtype=jnp.int32)
    same = (flat[:, None] == flat[None, :]) & (order[None, :] < order[:, None])
    position = jnp.sum(same.astype(jnp.int32), axis=1)
    return flat, position


def local(features, cross_weight, cross_bias, expert_ids, route_gates, expert_weight, mixed_grad):
    row_at = lax.axis_index("row")
    z_at = lax.axis_index("z")
    xh_at = lax.axis_index("xh")
    core_at = lax.axis_index("core")
    batch, block = features.shape
    width = cross_weight.shape[0]
    half = width // 2
    rows = expert_ids.shape[0]
    out_width = expert_weight.shape[2]
    share = out_width // ROWS_N
    slots = COL_N * CAP

    plane_there = (3 * z_at + row_at) % Z_N
    pieces = []
    for turn in range(2):
        perm = []
        for r in range(ROWS_N):
            for z in range(Z_N):
                for u in range(XH_N):
                    for v in range(CORE_N):
                        src = ((r * Z_N + z) * XH_N + u) * CORE_N + v
                        dst = ((z * Z_N + (3 * z + r) % Z_N) * XH_N + (v ^ turn)) * CORE_N + u
                        perm.append((src, dst))
        chip_there = plane_there * XH_N + (core_at ^ turn)
        pieces.append(lax.ppermute(piece(features, chip_there, 2 * rows), ALL, perm))

    features_there = swap(features, "core")
    weight_there = swap(cross_weight, "core")
    at = jnp.stack([core_at, xh_at]).astype(jnp.int32)
    early, late_own, late_other = cross_products(
        at, features, features_there, cross_weight, weight_there
    )
    early, pieces = lax.optimization_barrier((early, pieces))
    part = lax.psum_scatter(early, "z", scatter_dimension=0, tiled=True)
    late_sum = (
        late_own.astype(jnp.float32) + swap(late_other, "xh").astype(jnp.float32)
    ).astype(jnp.bfloat16)

    first = xh_at == 0
    base = jnp.concatenate(
        [jnp.where(first, pieces[0], pieces[1]), jnp.where(first, pieces[1], pieces[0])], axis=1
    ).astype(jnp.float32)

    ids_there = swap(expert_ids, "core")
    flat, position = slot_targets(expert_ids)
    flat_there, position_there = slot_targets(ids_there)
    places = jnp.arange(slots, dtype=jnp.int32)
    target = flat * CAP + position
    table = (places[:, None] == target[None, :]).astype(jnp.bfloat16)
    chooser = jnp.sum(table.reshape(slots, rows, 2), axis=2)
    chip_places = jnp.arange(2 * slots, dtype=jnp.int32)
    here = flat * (2 * CAP) + core_at * CAP + position
    there = flat_there * (2 * CAP) + (1 - core_at) * CAP + position_there
    chip_target = jnp.where(
        core_at == 0, jnp.concatenate([here, there]), jnp.concatenate([there, here])
    )
    chip_chooser = jnp.sum(
        (chip_places[:, None] == chip_target[None, :])
        .astype(jnp.bfloat16)
        .reshape(2 * slots, 2 * rows, 2),
        axis=2,
    )

    grad_share = piece(mixed_grad, row_at, share, 1).astype(jnp.float32)
    route_grad = (route_gates[:, :, None] * grad_share[:, None, :]).astype(jnp.bfloat16)
    send_grad = jnp.dot(
        table, route_grad.reshape(2 * rows, share), preferred_element_type=jnp.float32
    ).astype(jnp.bfloat16)
    lanes = share // 2
    send_grad = send_grad.reshape(COL_N, CAP, share)
    send_grad = jnp.concatenate([send_grad[:, :, :lanes], send_grad[:, :, lanes:]], axis=1)

    late_parts = lax.all_to_all(late_sum, "z", split_axis=0, concat_axis=0, tiled=True)
    part_there = swap(piece(part, 1 - xh_at, 2 * rows), "xh")
    late_parts, part_there, base, chip_chooser, chooser, table, send_grad = (
        lax.optimization_barrier(
            (late_parts, part_there, base, chip_chooser, chooser, table, send_grad)
        )
    )
    crossed_late = jnp.sum(late_parts.astype(jnp.float32), axis=0)
    crossed_early = piece(part, xh_at, 2 * rows).astype(jnp.float32) + part_there.astype(
        jnp.float32
    )
    crossed = jnp.concatenate([crossed_early, crossed_late], axis=1)
    bias = piece(cross_bias, core_at, half)
    hidden = (base * (crossed + bias) + base).astype(jnp.bfloat16)
    send_rows = jnp.dot(chip_chooser, hidden, preferred_element_type=jnp.float32).astype(
        jnp.bfloat16
    )
    send = jnp.concatenate([send_rows.reshape(COL_N, 2 * CAP, half), send_grad], axis=2)
    routed = lax.all_to_all(send, COL, split_axis=0, concat_axis=0, tiled=True)
    grad = routed[:, :, half:]
    routed_grad = jnp.concatenate([grad[:, :CAP], grad[:, CAP:]], axis=2).reshape(slots, share)
    routed = routed.reshape(COL_N // 2, 2, 2 * CAP, half + lanes)

    weight = expert_weight[0]
    pre = expert_call(forward_kernel, (ROWS_N, slots, share), routed, weight)
    parts = lax.all_to_all(pre, "row", split_axis=0, concat_axis=0, tiled=True)
    preact = jnp.sum(parts.astype(jnp.float32), axis=0)
    sigma = jax.nn.sigmoid(preact)
    activated = (preact * sigma).astype(jnp.bfloat16)
    slope = (
        routed_grad.astype(jnp.float32) * (sigma * (1.0 + preact * (1.0 - sigma)))
    ).astype(jnp.bfloat16)
    slopes = lax.all_to_all(
        jnp.broadcast_to(slope[None], (ROWS_N, slots, share)),
        "row",
        split_axis=0,
        concat_axis=0,
        tiled=True,
    )
    answer = expert_call(back_kernel, (slots, width + share), slopes, activated, weight)

    returned = lax.all_to_all(
        answer.reshape(COL_N, CAP, width + share), COL, split_axis=0, concat_axis=0, tiled=True
    ).reshape(slots, width + share)
    pull = (((0,), (0,)), ((), ()))
    pair_act = lax.dot_general(
        table, returned[:, width:], pull, preferred_element_type=jnp.float32
    )
    combined = jnp.sum(
        route_gates[:, :, None] * pair_act.reshape(rows, 2, share), axis=1
    ).astype(jnp.bfloat16)
    cross_grad = lax.dot_general(
        chooser, returned[:, :width], pull, preferred_element_type=jnp.float32
    ).astype(jnp.bfloat16)
    return combined, cross_grad


def solution(mesh):
    split = Mesh(mesh.devices.reshape(ROWS_N, Z_N, XH_N, CORE_N), ALL)
    return jax.shard_map(
        local,
        mesh=split,
        in_specs=(
            P(None, COL),
            P("row", COL),
            P("row"),
            P(COL, None),
            P(COL, None),
            P(COL, "row", None),
            P(COL, None),
        ),
        out_specs=(P(COL, "row"), P(COL, "row")),
        check_vma=False,
    )
```

```python
import jax
import jax.numpy as jnp
from jax import lax
from jax.experimental import pallas as pl
from jax.experimental.pallas import tpu as pltpu
from jax.sharding import Mesh, PartitionSpec as P

COL = ("z", "xh", "core")
ALL = ("row", "z", "xh", "core")
ROWS_N, Z_N, XH_N, CORE_N = 8, 8, 2, 2
COL_N = Z_N * XH_N * CORE_N
CAP = 8


def swap(values, axis):
    return lax.ppermute(values, axis, [(0, 1), (1, 0)])


def piece(values, index, size, axis=0):
    return lax.dynamic_slice_in_dim(values, index * size, size, axis)


GRANT = 56 << 20
CHUNKS, CUTS = 4, 4
NT = (((1,), (1,)), ((), ()))
VMEM = pl.BlockSpec(memory_space=pltpu.VMEM)


def dot_nt(left, right):
    return lax.dot_general(left, right, NT, preferred_element_type=jnp.float32)


def send_kernel(first, left, right, here, there, bias, chooser, out):
    block = left.shape[1]
    swapped = first[0] == 0
    for index in range(2):
        columns = slice(index * block, (index + 1) * block)
        straight, crosswise = (left, right) if index == 0 else (right, left)
        base = jnp.where(swapped, crosswise[...], straight[...]).astype(jnp.float32)
        crossed = here[:, columns].astype(jnp.float32) + there[:, columns].astype(jnp.float32)
        hidden = (base * (crossed + bias[:, columns]) + base).astype(jnp.bfloat16)
        out[:, columns] = jnp.dot(
            chooser[...], hidden, preferred_element_type=jnp.float32
        ).astype(jnp.bfloat16)


def send_rows_of(first, left, right, here, there, bias, chooser):
    return pl.pallas_call(
        send_kernel,
        in_specs=[pl.BlockSpec(memory_space=pltpu.SMEM)] + [VMEM] * 6,
        out_specs=VMEM,
        out_shape=jax.ShapeDtypeStruct((chooser.shape[0], here.shape[1]), jnp.bfloat16),
        cost_estimate=pl.CostEstimate(
            flops=2 * chooser.size * here.shape[1], bytes_accessed=2 << 20, transcendentals=0
        ),
        compiler_params=pltpu.CompilerParams(vmem_limit_bytes=24 << 20),
    )(first, left, right, here, there, bias, chooser)


def weight_copies(source, held, semaphores, by_columns):
    rows, columns = source.shape
    copies = []
    for chunk in range(CHUNKS):
        for cut in range(CUTS):
            if by_columns:
                part = (
                    pl.ds(cut * (rows // CUTS), rows // CUTS),
                    pl.ds(chunk * (columns // CHUNKS), columns // CHUNKS),
                )
            else:
                part = (pl.ds((chunk * CUTS + cut) * (rows // CHUNKS // CUTS), rows // CHUNKS // CUTS),)
            copies.append(
                pltpu.make_async_copy(
                    source.at[part], held.at[part], semaphores.at[chunk * CUTS + cut]
                )
            )
    return copies


def forward_kernel(routed, weight, out, held, semaphores):
    copies = weight_copies(weight, held, semaphores, True)
    for copy in copies:
        copy.start()
    shares, slots, share = out.shape
    half = held.shape[0] // 2
    wide = held.shape[1] // CHUNKS
    low = routed[:, 0, :, :half].reshape(slots, half)
    high = routed[:, 1, :, :half].reshape(slots, half)
    for chunk in range(CHUNKS):
        for copy in copies[chunk * CUTS : (chunk + 1) * CUTS]:
            copy.wait()
        columns = slice(chunk * wide, (chunk + 1) * wide)
        values = jnp.dot(low, held[:half, columns], preferred_element_type=jnp.float32)
        values += jnp.dot(high, held[half:, columns], preferred_element_type=jnp.float32)
        values = values.astype(jnp.bfloat16)
        for index in range(wide // share):
            out[chunk * (wide // share) + index] = values[:, index * share : (index + 1) * share]


def back_kernel(slopes, activated, weight, out, held, semaphores):
    copies = weight_copies(weight, held, semaphores, False)
    for copy in copies:
        copy.start()
    shares, slots, share = slopes.shape
    width = held.shape[0]
    tall = width // CHUNKS
    out[:, width:] = activated[...]
    for chunk in range(CHUNKS):
        for copy in copies[chunk * CUTS : (chunk + 1) * CUTS]:
            copy.wait()
        rows = slice(chunk * tall, (chunk + 1) * tall)
        values = jnp.zeros((slots, tall), jnp.float32)
        for index in range(shares):
            values += dot_nt(slopes[index], held[rows, index * share : (index + 1) * share])
        out[:, rows] = values.astype(jnp.bfloat16)


def expert_call(kernel, out_shape, *operands):
    weight = operands[-1]
    return pl.pallas_call(
        kernel,
        in_specs=[VMEM] * (len(operands) - 1) + [pl.BlockSpec(memory_space=pl.ANY)],
        out_specs=VMEM,
        out_shape=jax.ShapeDtypeStruct(out_shape, jnp.bfloat16),
        scratch_shapes=[
            pltpu.VMEM(weight.shape, weight.dtype),
            pltpu.SemaphoreType.DMA((CHUNKS * CUTS,)),
        ],
        compiler_params=pltpu.CompilerParams(vmem_limit_bytes=GRANT),
        cost_estimate=pl.CostEstimate(
            flops=2 * COL_N * CAP * weight.size, bytes_accessed=10 << 20, transcendentals=0
        ),
    )(*operands)


def slot_targets(expert_ids):
    flat = expert_ids.reshape(-1)
    count = flat.shape[0]
    order = jnp.arange(count, dtype=jnp.int32)
    same = (flat[:, None] == flat[None, :]) & (order[None, :] < order[:, None])
    position = jnp.sum(same.astype(jnp.int32), axis=1)
    return flat, position


def local(features, cross_weight, cross_bias, expert_ids, route_gates, expert_weight, mixed_grad):
    row_at = lax.axis_index("row")
    z_at = lax.axis_index("z")
    xh_at = lax.axis_index("xh")
    core_at = lax.axis_index("core")
    batch, block = features.shape
    width = cross_weight.shape[0]
    half = width // 2
    rows = expert_ids.shape[0]
    out_width = expert_weight.shape[2]
    share = out_width // ROWS_N
    slots = COL_N * CAP

    features_there = swap(features, "core")
    weight_there = swap(piece(cross_weight, 1 - core_at, half), "core")
    products = lax.dot_general(
        features, piece(cross_weight, core_at, half), NT, preferred_element_type=jnp.float32
    )
    products = products + lax.dot_general(
        features_there, weight_there, NT, preferred_element_type=jnp.float32
    )
    products, held_features, held_grad = lax.optimization_barrier(
        (products.astype(jnp.bfloat16), features, mixed_grad)
    )
    part = lax.psum_scatter(products, "z", scatter_dimension=0, tiled=True)

    plane_there = (3 * z_at + row_at) % Z_N
    pieces = []
    for turn in range(2):
        perm = []
        for r in range(ROWS_N):
            for z in range(Z_N):
                for u in range(XH_N):
                    for v in range(CORE_N):
                        src = ((r * Z_N + z) * XH_N + u) * CORE_N + v
                        dst = ((z * Z_N + (3 * z + r) % Z_N) * XH_N + (v ^ turn)) * CORE_N + u
                        perm.append((src, dst))
        chip_there = plane_there * XH_N + (core_at ^ turn)
        pieces.append(lax.ppermute(piece(held_features, chip_there, 2 * rows), ALL, perm))

    ids_there = swap(expert_ids, "core")
    flat, position = slot_targets(expert_ids)
    flat_there, position_there = slot_targets(ids_there)
    places = jnp.arange(slots, dtype=jnp.int32)
    target = flat * CAP + position
    table = (places[:, None] == target[None, :]).astype(jnp.bfloat16)
    chooser = jnp.sum(table.reshape(slots, rows, 2), axis=2)
    chip_places = jnp.arange(2 * slots, dtype=jnp.int32)
    here = flat * (2 * CAP) + core_at * CAP + position
    there = flat_there * (2 * CAP) + (1 - core_at) * CAP + position_there
    chip_target = jnp.where(
        core_at == 0, jnp.concatenate([here, there]), jnp.concatenate([there, here])
    )
    chip_chooser = jnp.sum(
        (chip_places[:, None] == chip_target[None, :])
        .astype(jnp.bfloat16)
        .reshape(2 * slots, 2 * rows, 2),
        axis=2,
    )

    grad_share = piece(held_grad, row_at, share, 1).astype(jnp.float32)
    route_grad = (route_gates[:, :, None] * grad_share[:, None, :]).astype(jnp.bfloat16)
    send_grad = jnp.dot(
        table, route_grad.reshape(2 * rows, share), preferred_element_type=jnp.float32
    ).astype(jnp.bfloat16)
    routed_grad = lax.all_to_all(
        send_grad.reshape(COL_N, CAP, share), COL, split_axis=0, concat_axis=0, tiled=True
    ).reshape(slots, share)

    part, pieces, chip_chooser, chooser, table, routed_grad = lax.optimization_barrier(
        (part, pieces, chip_chooser, chooser, table, routed_grad)
    )
    part_there = swap(piece(part, 1 - xh_at, 2 * rows), "xh")
    part_here = piece(part, xh_at, 2 * rows)
    bias = piece(cross_bias, core_at, half).reshape(1, half)
    first = (xh_at == 0).astype(jnp.int32).reshape(1)
    send_rows = send_rows_of(first, *pieces, part_here, part_there, bias, chip_chooser)
    routed = lax.all_to_all(
        send_rows.reshape(COL_N, 2 * CAP, half), COL, split_axis=0, concat_axis=0, tiled=True
    ).reshape(COL_N // 2, 2, 2 * CAP, half)

    weight = expert_weight[0]
    pre = expert_call(forward_kernel, (ROWS_N, slots, share), routed, weight)
    parts = lax.all_to_all(pre, "row", split_axis=0, concat_axis=0, tiled=True)
    preact = jnp.sum(parts.astype(jnp.float32), axis=0)
    sigma = jax.nn.sigmoid(preact)
    activated = (preact * sigma).astype(jnp.bfloat16)
    slope = (
        routed_grad.astype(jnp.float32) * (sigma * (1.0 + preact * (1.0 - sigma)))
    ).astype(jnp.bfloat16)
    slopes = lax.all_to_all(
        jnp.broadcast_to(slope[None], (ROWS_N, slots, share)),
        "row",
        split_axis=0,
        concat_axis=0,
        tiled=True,
    )
    answer = expert_call(back_kernel, (slots, width + share), slopes, activated, weight)

    returned = lax.all_to_all(
        answer.reshape(COL_N, CAP, width + share), COL, split_axis=0, concat_axis=0, tiled=True
    ).reshape(slots, width + share)
    pull = (((0,), (0,)), ((), ()))
    pair_act = lax.dot_general(
        table, returned[:, width:], pull, preferred_element_type=jnp.float32
    )
    combined = jnp.sum(
        route_gates[:, :, None] * pair_act.reshape(rows, 2, share), axis=1
    ).astype(jnp.bfloat16)
    cross_grad = lax.dot_general(
        chooser, returned[:, :width], pull, preferred_element_type=jnp.float32
    ).astype(jnp.bfloat16)
    return combined, cross_grad


def solution(mesh):
    split = Mesh(mesh.devices.reshape(ROWS_N, Z_N, XH_N, CORE_N), ALL)
    return jax.shard_map(
        local,
        mesh=split,
        in_specs=(
            P(None, COL),
            P("row", COL),
            P("row"),
            P(COL, None),
            P(COL, None),
            P(COL, "row", None),
            P(COL, None),
        ),
        out_specs=(P(COL, "row"), P(COL, "row")),
        check_vma=False,
    )
```

```python
import jax
import jax.numpy as jnp
from jax import lax
from jax.experimental import pallas as pl
from jax.experimental.pallas import tpu as pltpu
from jax.sharding import Mesh, PartitionSpec as P

COL = ("z", "xh", "core")
ALL = ("row", "z", "xh", "core")
ROWS_N, Z_N, XH_N, CORE_N = 8, 8, 2, 2
COL_N = Z_N * XH_N * CORE_N
CAP = 8


def swap(values, axis):
    return lax.ppermute(values, axis, [(0, 1), (1, 0)])


def piece(values, index, size, axis=0):
    return lax.dynamic_slice_in_dim(values, index * size, size, axis)


EARLY = 768
GRANT = 56 << 20
CHUNKS, CUTS = 4, 4
NT = (((1,), (1,)), ((), ()))
VMEM = pl.BlockSpec(memory_space=pltpu.VMEM)


def dot_nt(left, right):
    return lax.dot_general(left, right, NT, preferred_element_type=jnp.float32)


def products_kernel(at, here, there, weight_here, weight_there, early, own, other):
    values = dot_nt(here[...], weight_here[...]) + dot_nt(there[...], weight_there[...])
    values = values.astype(jnp.bfloat16)
    first_width = early.shape[1]
    planes, rows, columns = own.shape
    early[...] = values[:, :first_width]
    late = values[:, first_width:].reshape(planes, 2, rows, columns)
    first = at[1] == 0

    @pl.when(first)
    def _():
        own[...] = late[:, 0]
        other[...] = late[:, 1]

    @pl.when(jnp.logical_not(first))
    def _():
        own[...] = late[:, 1]
        other[...] = late[:, 0]


def cross_products(at, features, features_there, weight_here, weight_there):
    batch, block = features.shape
    columns = weight_here.shape[0] // 2
    late = columns - EARLY
    steps = 4
    tile = batch // steps
    planes, half_plane = Z_N // steps, batch // Z_N // 2
    rows = pl.BlockSpec((tile, block), lambda i, at: (i, 0))
    weights = pl.BlockSpec((columns, block), lambda i, at: (at[0], 0))
    late_spec = pl.BlockSpec((planes, half_plane, late), lambda i, at: (i, 0, 0))
    late_shape = jax.ShapeDtypeStruct((Z_N, half_plane, late), jnp.bfloat16)
    return pl.pallas_call(
        products_kernel,
        grid_spec=pltpu.PrefetchScalarGridSpec(
            num_scalar_prefetch=1,
            grid=(steps,),
            in_specs=[rows, rows, weights, weights],
            out_specs=[pl.BlockSpec((tile, EARLY), lambda i, at: (i, 0)), late_spec, late_spec],
        ),
        out_shape=[jax.ShapeDtypeStruct((batch, EARLY), jnp.bfloat16), late_shape, late_shape],
        compiler_params=pltpu.CompilerParams(vmem_limit_bytes=GRANT),
        cost_estimate=pl.CostEstimate(
            flops=4 * batch * columns * block, bytes_accessed=10 << 20, transcendentals=0
        ),
    )(at, features, features_there, weight_here, weight_there)


def send_kernel(first, left, right, here, there, late, bias, chooser, grad, out):
    block = left.shape[1]
    swapped = first[0] == 0
    late_sum = jnp.sum(late[...].astype(jnp.float32), axis=0)
    early_sum = here[...].astype(jnp.float32) + there[...].astype(jnp.float32)
    crossed = jnp.concatenate([early_sum, late_sum], axis=1) + bias[...]
    experts, amount, _ = out.shape
    for index in range(2):
        columns = slice(index * block, (index + 1) * block)
        straight, crosswise = (left, right) if index == 0 else (right, left)
        base = jnp.where(swapped, crosswise[...], straight[...]).astype(jnp.float32)
        hidden = (base * crossed[:, columns] + base).astype(jnp.bfloat16)
        chosen = jnp.dot(chooser[...], hidden, preferred_element_type=jnp.float32)
        out[:, :, columns] = chosen.astype(jnp.bfloat16).reshape(experts, amount, block)
    out[:, :, 2 * block :] = grad[...]


def send_rows_of(first, left, right, here, there, late, bias, chooser, grad):
    width = bias.shape[1] + grad.shape[2]
    return pl.pallas_call(
        send_kernel,
        in_specs=[pl.BlockSpec(memory_space=pltpu.SMEM)] + [VMEM] * 8,
        out_specs=VMEM,
        out_shape=jax.ShapeDtypeStruct(grad.shape[:2] + (width,), jnp.bfloat16),
        cost_estimate=pl.CostEstimate(
            flops=2 * chooser.size * bias.size, bytes_accessed=2 << 20, transcendentals=0
        ),
        compiler_params=pltpu.CompilerParams(vmem_limit_bytes=24 << 20),
    )(first, left, right, here, there, late, bias, chooser, grad)


def weight_copies(source, held, semaphores, by_columns):
    rows, columns = source.shape
    copies = []
    for chunk in range(CHUNKS):
        for cut in range(CUTS):
            if by_columns:
                part = (
                    pl.ds(cut * (rows // CUTS), rows // CUTS),
                    pl.ds(chunk * (columns // CHUNKS), columns // CHUNKS),
                )
            else:
                part = (pl.ds((chunk * CUTS + cut) * (rows // CHUNKS // CUTS), rows // CHUNKS // CUTS),)
            copies.append(
                pltpu.make_async_copy(
                    source.at[part], held.at[part], semaphores.at[chunk * CUTS + cut]
                )
            )
    return copies


def forward_kernel(routed, weight, out, held, semaphores):
    copies = weight_copies(weight, held, semaphores, True)
    for copy in copies:
        copy.start()
    shares, slots, share = out.shape
    half = held.shape[0] // 2
    wide = held.shape[1] // CHUNKS
    low = routed[:, 0, :, :half].reshape(slots, half)
    high = routed[:, 1, :, :half].reshape(slots, half)
    for chunk in range(CHUNKS):
        for copy in copies[chunk * CUTS : (chunk + 1) * CUTS]:
            copy.wait()
        columns = slice(chunk * wide, (chunk + 1) * wide)
        values = jnp.dot(low, held[:half, columns], preferred_element_type=jnp.float32)
        values += jnp.dot(high, held[half:, columns], preferred_element_type=jnp.float32)
        values = values.astype(jnp.bfloat16)
        for index in range(wide // share):
            out[chunk * (wide // share) + index] = values[:, index * share : (index + 1) * share]


def back_kernel(slopes, activated, weight, out, held, semaphores):
    copies = weight_copies(weight, held, semaphores, False)
    for copy in copies:
        copy.start()
    shares, slots, share = slopes.shape
    width = held.shape[0]
    tall = width // CHUNKS
    out[:, width:] = activated[...]
    for chunk in range(CHUNKS):
        for copy in copies[chunk * CUTS : (chunk + 1) * CUTS]:
            copy.wait()
        rows = slice(chunk * tall, (chunk + 1) * tall)
        values = jnp.zeros((slots, tall), jnp.float32)
        for index in range(shares):
            values += dot_nt(slopes[index], held[rows, index * share : (index + 1) * share])
        out[:, rows] = values.astype(jnp.bfloat16)


def expert_call(kernel, out_shape, *operands):
    weight = operands[-1]
    return pl.pallas_call(
        kernel,
        in_specs=[VMEM] * (len(operands) - 1) + [pl.BlockSpec(memory_space=pl.ANY)],
        out_specs=VMEM,
        out_shape=jax.ShapeDtypeStruct(out_shape, jnp.bfloat16),
        scratch_shapes=[
            pltpu.VMEM(weight.shape, weight.dtype),
            pltpu.SemaphoreType.DMA((CHUNKS * CUTS,)),
        ],
        compiler_params=pltpu.CompilerParams(vmem_limit_bytes=GRANT),
        cost_estimate=pl.CostEstimate(
            flops=2 * COL_N * CAP * weight.size, bytes_accessed=10 << 20, transcendentals=0
        ),
    )(*operands)


def slot_targets(expert_ids):
    flat = expert_ids.reshape(-1)
    count = flat.shape[0]
    order = jnp.arange(count, dtype=jnp.int32)
    same = (flat[:, None] == flat[None, :]) & (order[None, :] < order[:, None])
    position = jnp.sum(same.astype(jnp.int32), axis=1)
    return flat, position


def local(features, cross_weight, cross_bias, expert_ids, route_gates, expert_weight, mixed_grad):
    row_at = lax.axis_index("row")
    z_at = lax.axis_index("z")
    xh_at = lax.axis_index("xh")
    core_at = lax.axis_index("core")
    batch, block = features.shape
    width = cross_weight.shape[0]
    half = width // 2
    rows = expert_ids.shape[0]
    out_width = expert_weight.shape[2]
    share = out_width // ROWS_N
    slots = COL_N * CAP

    features_there = swap(features, "core")
    weight_there = swap(cross_weight, "core")
    at = jnp.stack([core_at, xh_at]).astype(jnp.int32)
    early, late_own, late_other = cross_products(
        at, features, features_there, cross_weight, weight_there
    )
    early, held_features = lax.optimization_barrier((early, features))
    part = lax.psum_scatter(early, "z", scatter_dimension=0, tiled=True)
    late_sum = (
        late_own.astype(jnp.float32) + swap(late_other, "xh").astype(jnp.float32)
    ).astype(jnp.bfloat16)

    plane_there = (3 * z_at + row_at) % Z_N
    pieces = []
    for turn in range(2):
        perm = []
        for r in range(ROWS_N):
            for z in range(Z_N):
                for u in range(XH_N):
                    for v in range(CORE_N):
                        src = ((r * Z_N + z) * XH_N + u) * CORE_N + v
                        dst = ((z * Z_N + (3 * z + r) % Z_N) * XH_N + (v ^ turn)) * CORE_N + u
                        perm.append((src, dst))
        chip_there = plane_there * XH_N + (core_at ^ turn)
        pieces.append(lax.ppermute(piece(held_features, chip_there, 2 * rows), ALL, perm))

    ids_there = swap(expert_ids, "core")
    flat, position = slot_targets(expert_ids)
    flat_there, position_there = slot_targets(ids_there)
    places = jnp.arange(slots, dtype=jnp.int32)
    target = flat * CAP + position
    table = (places[:, None] == target[None, :]).astype(jnp.bfloat16)
    chooser = jnp.sum(table.reshape(slots, rows, 2), axis=2)
    chip_places = jnp.arange(2 * slots, dtype=jnp.int32)
    here = flat * (2 * CAP) + core_at * CAP + position
    there = flat_there * (2 * CAP) + (1 - core_at) * CAP + position_there
    chip_target = jnp.where(
        core_at == 0, jnp.concatenate([here, there]), jnp.concatenate([there, here])
    )
    chip_chooser = jnp.sum(
        (chip_places[:, None] == chip_target[None, :])
        .astype(jnp.bfloat16)
        .reshape(2 * slots, 2 * rows, 2),
        axis=2,
    )

    grad_share = piece(mixed_grad, row_at, share, 1).astype(jnp.float32)
    route_grad = (route_gates[:, :, None] * grad_share[:, None, :]).astype(jnp.bfloat16)
    send_grad = jnp.dot(
        table, route_grad.reshape(2 * rows, share), preferred_element_type=jnp.float32
    ).astype(jnp.bfloat16)
    lanes = share // 2
    send_grad = send_grad.reshape(COL_N, CAP, share)
    send_grad = jnp.concatenate([send_grad[:, :, :lanes], send_grad[:, :, lanes:]], axis=1)

    late_sum, pieces = lax.optimization_barrier((late_sum, pieces))
    late_parts = lax.all_to_all(late_sum, "z", split_axis=0, concat_axis=0, tiled=True)
    part_there = swap(piece(part, 1 - xh_at, 2 * rows), "xh")
    late_parts, part_there, pieces, chip_chooser, chooser, table, send_grad = (
        lax.optimization_barrier(
            (late_parts, part_there, pieces, chip_chooser, chooser, table, send_grad)
        )
    )
    part_here = piece(part, xh_at, 2 * rows)
    bias = piece(cross_bias, core_at, half).reshape(1, half)
    first = (xh_at == 0).astype(jnp.int32).reshape(1)
    send = send_rows_of(
        first, *pieces, part_here, part_there, late_parts, bias, chip_chooser, send_grad
    )
    routed = lax.all_to_all(send, COL, split_axis=0, concat_axis=0, tiled=True)
    grad = routed[:, :, half:]
    routed_grad = jnp.concatenate([grad[:, :CAP], grad[:, CAP:]], axis=2).reshape(slots, share)
    routed = routed.reshape(COL_N // 2, 2, 2 * CAP, half + lanes)

    weight = expert_weight[0]
    pre = expert_call(forward_kernel, (ROWS_N, slots, share), routed, weight)
    parts = lax.all_to_all(pre, "row", split_axis=0, concat_axis=0, tiled=True)
    preact = jnp.sum(parts.astype(jnp.float32), axis=0)
    sigma = jax.nn.sigmoid(preact)
    activated = (preact * sigma).astype(jnp.bfloat16)
    slope = (
        routed_grad.astype(jnp.float32) * (sigma * (1.0 + preact * (1.0 - sigma)))
    ).astype(jnp.bfloat16)
    slopes = lax.all_to_all(
        jnp.broadcast_to(slope[None], (ROWS_N, slots, share)),
        "row",
        split_axis=0,
        concat_axis=0,
        tiled=True,
    )
    answer = expert_call(back_kernel, (slots, width + share), slopes, activated, weight)

    returned = lax.all_to_all(
        answer.reshape(COL_N, CAP, width + share), COL, split_axis=0, concat_axis=0, tiled=True
    ).reshape(slots, width + share)
    pull = (((0,), (0,)), ((), ()))
    pair_act = lax.dot_general(
        table, returned[:, width:], pull, preferred_element_type=jnp.float32
    )
    combined = jnp.sum(
        route_gates[:, :, None] * pair_act.reshape(rows, 2, share), axis=1
    ).astype(jnp.bfloat16)
    cross_grad = lax.dot_general(
        chooser, returned[:, :width], pull, preferred_element_type=jnp.float32
    ).astype(jnp.bfloat16)
    return combined, cross_grad


def solution(mesh):
    split = Mesh(mesh.devices.reshape(ROWS_N, Z_N, XH_N, CORE_N), ALL)
    return jax.shard_map(
        local,
        mesh=split,
        in_specs=(
            P(None, COL),
            P("row", COL),
            P("row"),
            P(COL, None),
            P(COL, None),
            P(COL, "row", None),
            P(COL, None),
        ),
        out_specs=(P(COL, "row"), P(COL, "row")),
        check_vma=False,
    )
```

```python
import jax
import jax.numpy as jnp
from jax import lax
from jax.experimental import pallas as pl
from jax.experimental.pallas import tpu as pltpu
from jax.sharding import Mesh, PartitionSpec as P

COL = ("z", "xh", "core")
ALL = ("row", "z", "xh", "core")
ROWS_N, Z_N, XH_N, CORE_N = 8, 8, 2, 2
COL_N = Z_N * XH_N * CORE_N
CAP = 8


def swap(values, axis):
    return lax.ppermute(values, axis, [(0, 1), (1, 0)])


def piece(values, index, size, axis=0):
    return lax.dynamic_slice_in_dim(values, index * size, size, axis)


GRANT = 56 << 20
CHUNKS, CUTS = 4, 4
NT = (((1,), (1,)), ((), ()))
VMEM = pl.BlockSpec(memory_space=pltpu.VMEM)


def dot_nt(left, right):
    return lax.dot_general(left, right, NT, preferred_element_type=jnp.float32)


def send_kernel(first, left, right, here, there, bias, chooser, out):
    block = left.shape[1]
    swapped = first[0] == 0
    for index in range(2):
        columns = slice(index * block, (index + 1) * block)
        straight, crosswise = (left, right) if index == 0 else (right, left)
        base = jnp.where(swapped, crosswise[...], straight[...]).astype(jnp.float32)
        crossed = here[:, columns].astype(jnp.float32) + there[:, columns].astype(jnp.float32)
        hidden = (base * (crossed + bias[:, columns]) + base).astype(jnp.bfloat16)
        out[:, columns] = jnp.dot(
            chooser[...], hidden, preferred_element_type=jnp.float32
        ).astype(jnp.bfloat16)


def send_rows_of(first, left, right, here, there, bias, chooser):
    return pl.pallas_call(
        send_kernel,
        in_specs=[pl.BlockSpec(memory_space=pltpu.SMEM)] + [VMEM] * 6,
        out_specs=VMEM,
        out_shape=jax.ShapeDtypeStruct((chooser.shape[0], here.shape[1]), jnp.bfloat16),
        cost_estimate=pl.CostEstimate(
            flops=2 * chooser.size * here.shape[1], bytes_accessed=2 << 20, transcendentals=0
        ),
        compiler_params=pltpu.CompilerParams(vmem_limit_bytes=24 << 20),
    )(first, left, right, here, there, bias, chooser)


def weight_copies(source, held, semaphores, by_columns):
    rows, columns = source.shape
    copies = []
    for chunk in range(CHUNKS):
        for cut in range(CUTS):
            if by_columns:
                part = (
                    pl.ds(cut * (rows // CUTS), rows // CUTS),
                    pl.ds(chunk * (columns // CHUNKS), columns // CHUNKS),
                )
            else:
                part = (pl.ds((chunk * CUTS + cut) * (rows // CHUNKS // CUTS), rows // CHUNKS // CUTS),)
            copies.append(
                pltpu.make_async_copy(
                    source.at[part], held.at[part], semaphores.at[chunk * CUTS + cut]
                )
            )
    return copies


def forward_kernel(routed, weight, out, held, semaphores):
    copies = weight_copies(weight, held, semaphores, True)
    for copy in copies:
        copy.start()
    shares, slots, share = out.shape
    half = held.shape[0] // 2
    wide = held.shape[1] // CHUNKS
    low = routed[:, 0, :, :half].reshape(slots, half)
    high = routed[:, 1, :, :half].reshape(slots, half)
    for chunk in range(CHUNKS):
        for copy in copies[chunk * CUTS : (chunk + 1) * CUTS]:
            copy.wait()
        columns = slice(chunk * wide, (chunk + 1) * wide)
        values = jnp.dot(low, held[:half, columns], preferred_element_type=jnp.float32)
        values += jnp.dot(high, held[half:, columns], preferred_element_type=jnp.float32)
        values = values.astype(jnp.bfloat16)
        for index in range(wide // share):
            out[chunk * (wide // share) + index] = values[:, index * share : (index + 1) * share]


def back_kernel(slopes, activated, weight, out, held, semaphores):
    copies = weight_copies(weight, held, semaphores, False)
    for copy in copies:
        copy.start()
    shares, slots, share = slopes.shape
    width = held.shape[0]
    tall = width // CHUNKS
    out[:, width:] = activated[...]
    for chunk in range(CHUNKS):
        for copy in copies[chunk * CUTS : (chunk + 1) * CUTS]:
            copy.wait()
        rows = slice(chunk * tall, (chunk + 1) * tall)
        values = jnp.zeros((slots, tall), jnp.float32)
        for index in range(shares):
            values += dot_nt(slopes[index], held[rows, index * share : (index + 1) * share])
        out[:, rows] = values.astype(jnp.bfloat16)


def expert_call(kernel, out_shape, *operands):
    weight = operands[-1]
    return pl.pallas_call(
        kernel,
        in_specs=[VMEM] * (len(operands) - 1) + [pl.BlockSpec(memory_space=pl.ANY)],
        out_specs=VMEM,
        out_shape=jax.ShapeDtypeStruct(out_shape, jnp.bfloat16),
        scratch_shapes=[
            pltpu.VMEM(weight.shape, weight.dtype),
            pltpu.SemaphoreType.DMA((CHUNKS * CUTS,)),
        ],
        compiler_params=pltpu.CompilerParams(vmem_limit_bytes=GRANT),
        cost_estimate=pl.CostEstimate(
            flops=2 * COL_N * CAP * weight.size, bytes_accessed=10 << 20, transcendentals=0
        ),
    )(*operands)


def slot_targets(expert_ids):
    flat = expert_ids.reshape(-1)
    count = flat.shape[0]
    order = jnp.arange(count, dtype=jnp.int32)
    same = (flat[:, None] == flat[None, :]) & (order[None, :] < order[:, None])
    position = jnp.sum(same.astype(jnp.int32), axis=1)
    return flat, position


def local(features, cross_weight, cross_bias, expert_ids, route_gates, expert_weight, mixed_grad):
    row_at = lax.axis_index("row")
    z_at = lax.axis_index("z")
    xh_at = lax.axis_index("xh")
    core_at = lax.axis_index("core")
    batch, block = features.shape
    width = cross_weight.shape[0]
    half = width // 2
    rows = expert_ids.shape[0]
    out_width = expert_weight.shape[2]
    share = out_width // ROWS_N
    slots = COL_N * CAP

    features_there = swap(features, "core")
    weight_there = swap(piece(cross_weight, 1 - core_at, half), "core")
    products = lax.dot_general(
        features, piece(cross_weight, core_at, half), NT, preferred_element_type=jnp.float32
    )
    products = products + lax.dot_general(
        features_there, weight_there, NT, preferred_element_type=jnp.float32
    )
    products, held_features, held_grad = lax.optimization_barrier(
        (products.astype(jnp.bfloat16), features, mixed_grad)
    )
    part = lax.psum_scatter(products, "z", scatter_dimension=0, tiled=True)

    plane_there = (3 * z_at + row_at) % Z_N
    perm = [
        (r * Z_N + z, r * Z_N + (3 * z + r) % Z_N) for r in range(ROWS_N) for z in range(Z_N)
    ]
    plane = lax.ppermute(piece(held_features, plane_there, 4 * rows), ("row", "z"), perm)
    perm = []
    for r in range(ROWS_N):
        for z in range(Z_N):
            for u in range(XH_N):
                for v in range(CORE_N):
                    src = ((r * Z_N + z) * XH_N + u) * CORE_N + v
                    dst = ((3 * (z - r) % Z_N * Z_N + z) * XH_N + v) * CORE_N + u
                    perm.append((src, dst))
    plane = lax.ppermute(plane, ALL, perm)
    pieces = [piece(plane, xh_at, 2 * rows), swap(piece(plane, 1 - xh_at, 2 * rows), "xh")]

    ids_there = swap(expert_ids, "core")
    flat, position = slot_targets(expert_ids)
    flat_there, position_there = slot_targets(ids_there)
    places = jnp.arange(slots, dtype=jnp.int32)
    target = flat * CAP + position
    table = (places[:, None] == target[None, :]).astype(jnp.bfloat16)
    chooser = jnp.sum(table.reshape(slots, rows, 2), axis=2)
    chip_places = jnp.arange(2 * slots, dtype=jnp.int32)
    here = flat * (2 * CAP) + core_at * CAP + position
    there = flat_there * (2 * CAP) + (1 - core_at) * CAP + position_there
    chip_target = jnp.where(
        core_at == 0, jnp.concatenate([here, there]), jnp.concatenate([there, here])
    )
    chip_chooser = jnp.sum(
        (chip_places[:, None] == chip_target[None, :])
        .astype(jnp.bfloat16)
        .reshape(2 * slots, 2 * rows, 2),
        axis=2,
    )

    grad_share = piece(held_grad, row_at, share, 1).astype(jnp.float32)
    route_grad = (route_gates[:, :, None] * grad_share[:, None, :]).astype(jnp.bfloat16)
    send_grad = jnp.dot(
        table, route_grad.reshape(2 * rows, share), preferred_element_type=jnp.float32
    ).astype(jnp.bfloat16)
    routed_grad = lax.all_to_all(
        send_grad.reshape(COL_N, CAP, share), COL, split_axis=0, concat_axis=0, tiled=True
    ).reshape(slots, share)

    part, pieces, chip_chooser, chooser, table, routed_grad = lax.optimization_barrier(
        (part, pieces, chip_chooser, chooser, table, routed_grad)
    )
    part_there = swap(piece(part, 1 - xh_at, 2 * rows), "xh")
    part_here = piece(part, xh_at, 2 * rows)
    bias = piece(cross_bias, core_at, half).reshape(1, half)
    first = (xh_at == 0).astype(jnp.int32).reshape(1)
    send_rows = send_rows_of(first, *pieces, part_here, part_there, bias, chip_chooser)
    routed = lax.all_to_all(
        send_rows.reshape(COL_N, 2 * CAP, half), COL, split_axis=0, concat_axis=0, tiled=True
    ).reshape(COL_N // 2, 2, 2 * CAP, half)

    weight = expert_weight[0]
    pre = expert_call(forward_kernel, (ROWS_N, slots, share), routed, weight)
    parts = lax.all_to_all(pre, "row", split_axis=0, concat_axis=0, tiled=True)
    preact = jnp.sum(parts.astype(jnp.float32), axis=0)
    sigma = jax.nn.sigmoid(preact)
    activated = (preact * sigma).astype(jnp.bfloat16)
    slope = (
        routed_grad.astype(jnp.float32) * (sigma * (1.0 + preact * (1.0 - sigma)))
    ).astype(jnp.bfloat16)
    slopes = lax.all_to_all(
        jnp.broadcast_to(slope[None], (ROWS_N, slots, share)),
        "row",
        split_axis=0,
        concat_axis=0,
        tiled=True,
    )
    answer = expert_call(back_kernel, (slots, width + share), slopes, activated, weight)

    returned = lax.all_to_all(
        answer.reshape(COL_N, CAP, width + share), COL, split_axis=0, concat_axis=0, tiled=True
    ).reshape(slots, width + share)
    pull = (((0,), (0,)), ((), ()))
    pair_act = lax.dot_general(
        table, returned[:, width:], pull, preferred_element_type=jnp.float32
    )
    combined = jnp.sum(
        route_gates[:, :, None] * pair_act.reshape(rows, 2, share), axis=1
    ).astype(jnp.bfloat16)
    cross_grad = lax.dot_general(
        chooser, returned[:, :width], pull, preferred_element_type=jnp.float32
    ).astype(jnp.bfloat16)
    return combined, cross_grad


def solution(mesh):
    split = Mesh(mesh.devices.reshape(ROWS_N, Z_N, XH_N, CORE_N), ALL)
    return jax.shard_map(
        local,
        mesh=split,
        in_specs=(
            P(None, COL),
            P("row", COL),
            P("row"),
            P(COL, None),
            P(COL, None),
            P(COL, "row", None),
            P(COL, None),
        ),
        out_specs=(P(COL, "row"), P(COL, "row")),
        check_vma=False,
    )
```

```python
import jax
import jax.numpy as jnp
from jax import lax
from jax.experimental import pallas as pl
from jax.experimental.pallas import tpu as pltpu
from jax.sharding import Mesh, PartitionSpec as P

COL = ("z", "xh", "core")
ALL = ("row", "z", "xh", "core")
ROWS_N, Z_N, XH_N, CORE_N = 8, 8, 2, 2
COL_N = Z_N * XH_N * CORE_N
CAP = 8


def swap(values, axis):
    return lax.ppermute(values, axis, [(0, 1), (1, 0)])


def piece(values, index, size, axis=0):
    return lax.dynamic_slice_in_dim(values, index * size, size, axis)


EARLY = 512
GRANT = 56 << 20
CHUNKS, CUTS = 4, 4
NT = (((1,), (1,)), ((), ()))
VMEM = pl.BlockSpec(memory_space=pltpu.VMEM)


def dot_nt(left, right):
    return lax.dot_general(left, right, NT, preferred_element_type=jnp.float32)


def products_kernel(at, here, there, weight_here, weight_there, early, own, other):
    values = dot_nt(here[...], weight_here[...]) + dot_nt(there[...], weight_there[...])
    values = values.astype(jnp.bfloat16)
    first_width = early.shape[1]
    planes, rows, columns = own.shape
    early[...] = values[:, :first_width]
    late = values[:, first_width:].reshape(planes, 2, rows, columns)
    first = at[1] == 0

    @pl.when(first)
    def _():
        own[...] = late[:, 0]
        other[...] = late[:, 1]

    @pl.when(jnp.logical_not(first))
    def _():
        own[...] = late[:, 1]
        other[...] = late[:, 0]


def cross_products(at, features, features_there, weight_here, weight_there):
    batch, block = features.shape
    columns = weight_here.shape[0] // 2
    late = columns - EARLY
    steps = 4
    tile = batch // steps
    planes, half_plane = Z_N // steps, batch // Z_N // 2
    rows = pl.BlockSpec((tile, block), lambda i, at: (i, 0))
    weights = pl.BlockSpec((columns, block), lambda i, at: (at[0], 0))
    late_spec = pl.BlockSpec((planes, half_plane, late), lambda i, at: (i, 0, 0))
    late_shape = jax.ShapeDtypeStruct((Z_N, half_plane, late), jnp.bfloat16)
    return pl.pallas_call(
        products_kernel,
        grid_spec=pltpu.PrefetchScalarGridSpec(
            num_scalar_prefetch=1,
            grid=(steps,),
            in_specs=[rows, rows, weights, weights],
            out_specs=[pl.BlockSpec((tile, EARLY), lambda i, at: (i, 0)), late_spec, late_spec],
        ),
        out_shape=[jax.ShapeDtypeStruct((batch, EARLY), jnp.bfloat16), late_shape, late_shape],
        compiler_params=pltpu.CompilerParams(vmem_limit_bytes=GRANT),
        cost_estimate=pl.CostEstimate(
            flops=4 * batch * columns * block, bytes_accessed=10 << 20, transcendentals=0
        ),
    )(at, features, features_there, weight_here, weight_there)


def send_kernel(first, left, right, here, there, late, bias, chooser, grad, out):
    block = left.shape[1]
    swapped = first[0] == 0
    late_sum = jnp.sum(late[...].astype(jnp.float32), axis=0)
    early_sum = here[...].astype(jnp.float32) + there[...].astype(jnp.float32)
    crossed = jnp.concatenate([early_sum, late_sum], axis=1) + bias[...]
    experts, amount, _ = out.shape
    for index in range(2):
        columns = slice(index * block, (index + 1) * block)
        straight, crosswise = (left, right) if index == 0 else (right, left)
        base = jnp.where(swapped, crosswise[...], straight[...]).astype(jnp.float32)
        hidden = (base * crossed[:, columns] + base).astype(jnp.bfloat16)
        chosen = jnp.dot(chooser[...], hidden, preferred_element_type=jnp.float32)
        out[:, :, columns] = chosen.astype(jnp.bfloat16).reshape(experts, amount, block)
    out[:, :, 2 * block :] = grad[...]


def send_rows_of(first, left, right, here, there, late, bias, chooser, grad):
    width = bias.shape[1] + grad.shape[2]
    return pl.pallas_call(
        send_kernel,
        in_specs=[pl.BlockSpec(memory_space=pltpu.SMEM)] + [VMEM] * 8,
        out_specs=VMEM,
        out_shape=jax.ShapeDtypeStruct(grad.shape[:2] + (width,), jnp.bfloat16),
        cost_estimate=pl.CostEstimate(
            flops=2 * chooser.size * bias.size, bytes_accessed=2 << 20, transcendentals=0
        ),
        compiler_params=pltpu.CompilerParams(vmem_limit_bytes=24 << 20),
    )(first, left, right, here, there, late, bias, chooser, grad)


def weight_copies(source, held, semaphores, by_columns):
    rows, columns = source.shape
    copies = []
    for chunk in range(CHUNKS):
        for cut in range(CUTS):
            if by_columns:
                part = (
                    pl.ds(cut * (rows // CUTS), rows // CUTS),
                    pl.ds(chunk * (columns // CHUNKS), columns // CHUNKS),
                )
            else:
                part = (pl.ds((chunk * CUTS + cut) * (rows // CHUNKS // CUTS), rows // CHUNKS // CUTS),)
            copies.append(
                pltpu.make_async_copy(
                    source.at[part], held.at[part], semaphores.at[chunk * CUTS + cut]
                )
            )
    return copies


def forward_kernel(routed, weight, out, held, semaphores):
    copies = weight_copies(weight, held, semaphores, True)
    for copy in copies:
        copy.start()
    shares, slots, share = out.shape
    half = held.shape[0] // 2
    wide = held.shape[1] // CHUNKS
    low = routed[:, 0, :, :half].reshape(slots, half)
    high = routed[:, 1, :, :half].reshape(slots, half)
    for chunk in range(CHUNKS):
        for copy in copies[chunk * CUTS : (chunk + 1) * CUTS]:
            copy.wait()
        columns = slice(chunk * wide, (chunk + 1) * wide)
        values = jnp.dot(low, held[:half, columns], preferred_element_type=jnp.float32)
        values += jnp.dot(high, held[half:, columns], preferred_element_type=jnp.float32)
        values = values.astype(jnp.bfloat16)
        for index in range(wide // share):
            out[chunk * (wide // share) + index] = values[:, index * share : (index + 1) * share]


def back_kernel(slopes, activated, weight, out, held, semaphores):
    copies = weight_copies(weight, held, semaphores, False)
    for copy in copies:
        copy.start()
    shares, slots, share = slopes.shape
    width = held.shape[0]
    tall = width // CHUNKS
    out[:, width:] = activated[...]
    for chunk in range(CHUNKS):
        for copy in copies[chunk * CUTS : (chunk + 1) * CUTS]:
            copy.wait()
        rows = slice(chunk * tall, (chunk + 1) * tall)
        values = jnp.zeros((slots, tall), jnp.float32)
        for index in range(shares):
            values += dot_nt(slopes[index], held[rows, index * share : (index + 1) * share])
        out[:, rows] = values.astype(jnp.bfloat16)


def expert_call(kernel, out_shape, *operands):
    weight = operands[-1]
    return pl.pallas_call(
        kernel,
        in_specs=[VMEM] * (len(operands) - 1) + [pl.BlockSpec(memory_space=pl.ANY)],
        out_specs=VMEM,
        out_shape=jax.ShapeDtypeStruct(out_shape, jnp.bfloat16),
        scratch_shapes=[
            pltpu.VMEM(weight.shape, weight.dtype),
            pltpu.SemaphoreType.DMA((CHUNKS * CUTS,)),
        ],
        compiler_params=pltpu.CompilerParams(vmem_limit_bytes=GRANT),
        cost_estimate=pl.CostEstimate(
            flops=2 * COL_N * CAP * weight.size, bytes_accessed=10 << 20, transcendentals=0
        ),
    )(*operands)


def slot_targets(expert_ids):
    flat = expert_ids.reshape(-1)
    count = flat.shape[0]
    order = jnp.arange(count, dtype=jnp.int32)
    same = (flat[:, None] == flat[None, :]) & (order[None, :] < order[:, None])
    position = jnp.sum(same.astype(jnp.int32), axis=1)
    return flat, position


def local(features, cross_weight, cross_bias, expert_ids, route_gates, expert_weight, mixed_grad):
    row_at = lax.axis_index("row")
    z_at = lax.axis_index("z")
    xh_at = lax.axis_index("xh")
    core_at = lax.axis_index("core")
    batch, block = features.shape
    width = cross_weight.shape[0]
    half = width // 2
    rows = expert_ids.shape[0]
    out_width = expert_weight.shape[2]
    share = out_width // ROWS_N
    slots = COL_N * CAP

    features_there = swap(features, "core")
    weight_there = swap(cross_weight, "core")
    at = jnp.stack([core_at, xh_at]).astype(jnp.int32)
    early, late_own, late_other = cross_products(
        at, features, features_there, cross_weight, weight_there
    )
    early, held_features = lax.optimization_barrier((early, features))
    part = lax.psum_scatter(early, "z", scatter_dimension=0, tiled=True)
    late_sum = (
        late_own.astype(jnp.float32) + swap(late_other, "xh").astype(jnp.float32)
    ).astype(jnp.bfloat16)

    plane_there = (3 * z_at + row_at) % Z_N
    perm = [
        (r * Z_N + z, r * Z_N + (3 * z + r) % Z_N) for r in range(ROWS_N) for z in range(Z_N)
    ]
    plane = lax.ppermute(piece(held_features, plane_there, 4 * rows), ("row", "z"), perm)
    perm = []
    for r in range(ROWS_N):
        for z in range(Z_N):
            for u in range(XH_N):
                for v in range(CORE_N):
                    src = ((r * Z_N + z) * XH_N + u) * CORE_N + v
                    dst = ((3 * (z - r) % Z_N * Z_N + z) * XH_N + v) * CORE_N + u
                    perm.append((src, dst))
    plane = lax.ppermute(plane, ALL, perm)

    ids_there = swap(expert_ids, "core")
    flat, position = slot_targets(expert_ids)
    flat_there, position_there = slot_targets(ids_there)
    places = jnp.arange(slots, dtype=jnp.int32)
    target = flat * CAP + position
    table = (places[:, None] == target[None, :]).astype(jnp.bfloat16)
    chooser = jnp.sum(table.reshape(slots, rows, 2), axis=2)
    chip_places = jnp.arange(2 * slots, dtype=jnp.int32)
    here = flat * (2 * CAP) + core_at * CAP + position
    there = flat_there * (2 * CAP) + (1 - core_at) * CAP + position_there
    chip_target = jnp.where(
        core_at == 0, jnp.concatenate([here, there]), jnp.concatenate([there, here])
    )
    chip_chooser = jnp.sum(
        (chip_places[:, None] == chip_target[None, :])
        .astype(jnp.bfloat16)
        .reshape(2 * slots, 2 * rows, 2),
        axis=2,
    )

    grad_share = piece(mixed_grad, row_at, share, 1).astype(jnp.float32)
    route_grad = (route_gates[:, :, None] * grad_share[:, None, :]).astype(jnp.bfloat16)
    send_grad = jnp.dot(
        table, route_grad.reshape(2 * rows, share), preferred_element_type=jnp.float32
    ).astype(jnp.bfloat16)
    lanes = share // 2
    send_grad = send_grad.reshape(COL_N, CAP, share)
    send_grad = jnp.concatenate([send_grad[:, :, :lanes], send_grad[:, :, lanes:]], axis=1)

    late_sum, plane = lax.optimization_barrier((late_sum, plane))
    pieces = [piece(plane, xh_at, 2 * rows), swap(piece(plane, 1 - xh_at, 2 * rows), "xh")]
    late_parts = lax.all_to_all(late_sum, "z", split_axis=0, concat_axis=0, tiled=True)
    part_there = swap(piece(part, 1 - xh_at, 2 * rows), "xh")
    late_parts, part_there, pieces, chip_chooser, chooser, table, send_grad = (
        lax.optimization_barrier(
            (late_parts, part_there, pieces, chip_chooser, chooser, table, send_grad)
        )
    )
    part_here = piece(part, xh_at, 2 * rows)
    bias = piece(cross_bias, core_at, half).reshape(1, half)
    first = (xh_at == 0).astype(jnp.int32).reshape(1)
    send = send_rows_of(
        first, *pieces, part_here, part_there, late_parts, bias, chip_chooser, send_grad
    )
    routed = lax.all_to_all(send, COL, split_axis=0, concat_axis=0, tiled=True)
    grad = routed[:, :, half:]
    routed_grad = jnp.concatenate([grad[:, :CAP], grad[:, CAP:]], axis=2).reshape(slots, share)
    routed = routed.reshape(COL_N // 2, 2, 2 * CAP, half + lanes)

    weight = expert_weight[0]
    pre = expert_call(forward_kernel, (ROWS_N, slots, share), routed, weight)
    parts = lax.all_to_all(pre, "row", split_axis=0, concat_axis=0, tiled=True)
    preact = jnp.sum(parts.astype(jnp.float32), axis=0)
    sigma = jax.nn.sigmoid(preact)
    activated = (preact * sigma).astype(jnp.bfloat16)
    slope = (
        routed_grad.astype(jnp.float32) * (sigma * (1.0 + preact * (1.0 - sigma)))
    ).astype(jnp.bfloat16)
    slopes = lax.all_to_all(
        jnp.broadcast_to(slope[None], (ROWS_N, slots, share)),
        "row",
        split_axis=0,
        concat_axis=0,
        tiled=True,
    )
    answer = expert_call(back_kernel, (slots, width + share), slopes, activated, weight)

    returned = lax.all_to_all(
        answer.reshape(COL_N, CAP, width + share), COL, split_axis=0, concat_axis=0, tiled=True
    ).reshape(slots, width + share)
    pull = (((0,), (0,)), ((), ()))
    pair_act = lax.dot_general(
        table, returned[:, width:], pull, preferred_element_type=jnp.float32
    )
    combined = jnp.sum(
        route_gates[:, :, None] * pair_act.reshape(rows, 2, share), axis=1
    ).astype(jnp.bfloat16)
    cross_grad = lax.dot_general(
        chooser, returned[:, :width], pull, preferred_element_type=jnp.float32
    ).astype(jnp.bfloat16)
    return combined, cross_grad


def solution(mesh):
    split = Mesh(mesh.devices.reshape(ROWS_N, Z_N, XH_N, CORE_N), ALL)
    return jax.shard_map(
        local,
        mesh=split,
        in_specs=(
            P(None, COL),
            P("row", COL),
            P("row"),
            P(COL, None),
            P(COL, None),
            P(COL, "row", None),
            P(COL, None),
        ),
        out_specs=(P(COL, "row"), P(COL, "row")),
        check_vma=False,
    )
```

```python
import jax
import jax.numpy as jnp
from jax import lax
from jax.experimental import pallas as pl
from jax.experimental.pallas import tpu as pltpu
from jax.sharding import Mesh, PartitionSpec as P

COL = ("z", "xh", "core")
ALL = ("row", "z", "xh", "core")
ROWS_N, Z_N, XH_N, CORE_N = 8, 8, 2, 2
COL_N = Z_N * XH_N * CORE_N
CAP = 8


def swap(values, axis):
    return lax.ppermute(values, axis, [(0, 1), (1, 0)])


def piece(values, index, size, axis=0):
    return lax.dynamic_slice_in_dim(values, index * size, size, axis)


EARLY = 640
GRANT = 56 << 20
CHUNKS, CUTS = 4, 4
NT = (((1,), (1,)), ((), ()))
VMEM = pl.BlockSpec(memory_space=pltpu.VMEM)


def dot_nt(left, right):
    return lax.dot_general(left, right, NT, preferred_element_type=jnp.float32)


def products_kernel(at, here, there, weight_here, weight_there, early, own, other):
    values = dot_nt(here[...], weight_here[...]) + dot_nt(there[...], weight_there[...])
    values = values.astype(jnp.bfloat16)
    first_width = early.shape[1]
    planes, rows, columns = own.shape
    early[...] = values[:, :first_width]
    late = values[:, first_width:].reshape(planes, 2, rows, columns)
    first = at[1] == 0

    @pl.when(first)
    def _():
        own[...] = late[:, 0]
        other[...] = late[:, 1]

    @pl.when(jnp.logical_not(first))
    def _():
        own[...] = late[:, 1]
        other[...] = late[:, 0]


def cross_products(at, features, features_there, weight_here, weight_there):
    batch, block = features.shape
    columns = weight_here.shape[0] // 2
    late = columns - EARLY
    steps = 4
    tile = batch // steps
    planes, half_plane = Z_N // steps, batch // Z_N // 2
    rows = pl.BlockSpec((tile, block), lambda i, at: (i, 0))
    weights = pl.BlockSpec((columns, block), lambda i, at: (at[0], 0))
    late_spec = pl.BlockSpec((planes, half_plane, late), lambda i, at: (i, 0, 0))
    late_shape = jax.ShapeDtypeStruct((Z_N, half_plane, late), jnp.bfloat16)
    return pl.pallas_call(
        products_kernel,
        grid_spec=pltpu.PrefetchScalarGridSpec(
            num_scalar_prefetch=1,
            grid=(steps,),
            in_specs=[rows, rows, weights, weights],
            out_specs=[pl.BlockSpec((tile, EARLY), lambda i, at: (i, 0)), late_spec, late_spec],
        ),
        out_shape=[jax.ShapeDtypeStruct((batch, EARLY), jnp.bfloat16), late_shape, late_shape],
        compiler_params=pltpu.CompilerParams(vmem_limit_bytes=GRANT),
        cost_estimate=pl.CostEstimate(
            flops=4 * batch * columns * block, bytes_accessed=10 << 20, transcendentals=0
        ),
    )(at, features, features_there, weight_here, weight_there)


def send_kernel(first, left, right, here, there, late, bias, chooser, grad, out):
    block = left.shape[1]
    swapped = first[0] == 0
    late_sum = jnp.sum(late[...].astype(jnp.float32), axis=0)
    early_sum = here[...].astype(jnp.float32) + there[...].astype(jnp.float32)
    crossed = jnp.concatenate([early_sum, late_sum], axis=1) + bias[...]
    experts, amount, _ = out.shape
    for index in range(2):
        columns = slice(index * block, (index + 1) * block)
        straight, crosswise = (left, right) if index == 0 else (right, left)
        base = jnp.where(swapped, crosswise[...], straight[...]).astype(jnp.float32)
        hidden = (base * crossed[:, columns] + base).astype(jnp.bfloat16)
        chosen = jnp.dot(chooser[...], hidden, preferred_element_type=jnp.float32)
        out[:, :, columns] = chosen.astype(jnp.bfloat16).reshape(experts, amount, block)
    out[:, :, 2 * block :] = grad[...]


def send_rows_of(first, left, right, here, there, late, bias, chooser, grad):
    width = bias.shape[1] + grad.shape[2]
    return pl.pallas_call(
        send_kernel,
        in_specs=[pl.BlockSpec(memory_space=pltpu.SMEM)] + [VMEM] * 8,
        out_specs=VMEM,
        out_shape=jax.ShapeDtypeStruct(grad.shape[:2] + (width,), jnp.bfloat16),
        cost_estimate=pl.CostEstimate(
            flops=2 * chooser.size * bias.size, bytes_accessed=2 << 20, transcendentals=0
        ),
        compiler_params=pltpu.CompilerParams(vmem_limit_bytes=24 << 20),
    )(first, left, right, here, there, late, bias, chooser, grad)


def weight_copies(source, held, semaphores, by_columns):
    rows, columns = source.shape
    copies = []
    for chunk in range(CHUNKS):
        for cut in range(CUTS):
            if by_columns:
                part = (
                    pl.ds(cut * (rows // CUTS), rows // CUTS),
                    pl.ds(chunk * (columns // CHUNKS), columns // CHUNKS),
                )
            else:
                part = (pl.ds((chunk * CUTS + cut) * (rows // CHUNKS // CUTS), rows // CHUNKS // CUTS),)
            copies.append(
                pltpu.make_async_copy(
                    source.at[part], held.at[part], semaphores.at[chunk * CUTS + cut]
                )
            )
    return copies


def forward_kernel(routed, weight, out, held, semaphores):
    copies = weight_copies(weight, held, semaphores, True)
    for copy in copies:
        copy.start()
    shares, slots, share = out.shape
    half = held.shape[0] // 2
    wide = held.shape[1] // CHUNKS
    low = routed[:, 0, :, :half].reshape(slots, half)
    high = routed[:, 1, :, :half].reshape(slots, half)
    for chunk in range(CHUNKS):
        for copy in copies[chunk * CUTS : (chunk + 1) * CUTS]:
            copy.wait()
        columns = slice(chunk * wide, (chunk + 1) * wide)
        values = jnp.dot(low, held[:half, columns], preferred_element_type=jnp.float32)
        values += jnp.dot(high, held[half:, columns], preferred_element_type=jnp.float32)
        values = values.astype(jnp.bfloat16)
        for index in range(wide // share):
            out[chunk * (wide // share) + index] = values[:, index * share : (index + 1) * share]


def back_kernel(slopes, activated, weight, out, held, semaphores):
    copies = weight_copies(weight, held, semaphores, False)
    for copy in copies:
        copy.start()
    shares, slots, share = slopes.shape
    width = held.shape[0]
    tall = width // CHUNKS
    out[:, width:] = activated[...]
    for chunk in range(CHUNKS):
        for copy in copies[chunk * CUTS : (chunk + 1) * CUTS]:
            copy.wait()
        rows = slice(chunk * tall, (chunk + 1) * tall)
        values = jnp.zeros((slots, tall), jnp.float32)
        for index in range(shares):
            values += dot_nt(slopes[index], held[rows, index * share : (index + 1) * share])
        out[:, rows] = values.astype(jnp.bfloat16)


def expert_call(kernel, out_shape, *operands):
    weight = operands[-1]
    return pl.pallas_call(
        kernel,
        in_specs=[VMEM] * (len(operands) - 1) + [pl.BlockSpec(memory_space=pl.ANY)],
        out_specs=VMEM,
        out_shape=jax.ShapeDtypeStruct(out_shape, jnp.bfloat16),
        scratch_shapes=[
            pltpu.VMEM(weight.shape, weight.dtype),
            pltpu.SemaphoreType.DMA((CHUNKS * CUTS,)),
        ],
        compiler_params=pltpu.CompilerParams(vmem_limit_bytes=GRANT),
        cost_estimate=pl.CostEstimate(
            flops=2 * COL_N * CAP * weight.size, bytes_accessed=10 << 20, transcendentals=0
        ),
    )(*operands)


def slot_targets(expert_ids):
    flat = expert_ids.reshape(-1)
    count = flat.shape[0]
    order = jnp.arange(count, dtype=jnp.int32)
    same = (flat[:, None] == flat[None, :]) & (order[None, :] < order[:, None])
    position = jnp.sum(same.astype(jnp.int32), axis=1)
    return flat, position


def local(features, cross_weight, cross_bias, expert_ids, route_gates, expert_weight, mixed_grad):
    row_at = lax.axis_index("row")
    z_at = lax.axis_index("z")
    xh_at = lax.axis_index("xh")
    core_at = lax.axis_index("core")
    batch, block = features.shape
    width = cross_weight.shape[0]
    half = width // 2
    rows = expert_ids.shape[0]
    out_width = expert_weight.shape[2]
    share = out_width // ROWS_N
    slots = COL_N * CAP

    features_there = swap(features, "core")
    weight_there = swap(cross_weight, "core")
    at = jnp.stack([core_at, xh_at]).astype(jnp.int32)
    early, late_own, late_other = cross_products(
        at, features, features_there, cross_weight, weight_there
    )
    early, held_features = lax.optimization_barrier((early, features))
    part = lax.psum_scatter(early, "z", scatter_dimension=0, tiled=True)
    late_sum = (
        late_own.astype(jnp.float32) + swap(late_other, "xh").astype(jnp.float32)
    ).astype(jnp.bfloat16)

    plane_there = (3 * z_at + row_at) % Z_N
    perm = [
        (r * Z_N + z, r * Z_N + (3 * z + r) % Z_N) for r in range(ROWS_N) for z in range(Z_N)
    ]
    plane = lax.ppermute(piece(held_features, plane_there, 4 * rows), ("row", "z"), perm)
    ids_there = swap(expert_ids, "core")
    flat, position = slot_targets(expert_ids)
    flat_there, position_there = slot_targets(ids_there)
    places = jnp.arange(slots, dtype=jnp.int32)
    target = flat * CAP + position
    table = (places[:, None] == target[None, :]).astype(jnp.bfloat16)
    chooser = jnp.sum(table.reshape(slots, rows, 2), axis=2)
    chip_places = jnp.arange(2 * slots, dtype=jnp.int32)
    here = flat * (2 * CAP) + core_at * CAP + position
    there = flat_there * (2 * CAP) + (1 - core_at) * CAP + position_there
    chip_target = jnp.where(
        core_at == 0, jnp.concatenate([here, there]), jnp.concatenate([there, here])
    )
    chip_chooser = jnp.sum(
        (chip_places[:, None] == chip_target[None, :])
        .astype(jnp.bfloat16)
        .reshape(2 * slots, 2 * rows, 2),
        axis=2,
    )

    grad_share = piece(mixed_grad, row_at, share, 1).astype(jnp.float32)
    route_grad = (route_gates[:, :, None] * grad_share[:, None, :]).astype(jnp.bfloat16)
    send_grad = jnp.dot(
        table, route_grad.reshape(2 * rows, share), preferred_element_type=jnp.float32
    ).astype(jnp.bfloat16)
    lanes = share // 2
    send_grad = send_grad.reshape(COL_N, CAP, share)
    send_grad = jnp.concatenate([send_grad[:, :, :lanes], send_grad[:, :, lanes:]], axis=1)

    late_sum, plane = lax.optimization_barrier((late_sum, plane))
    perm = []
    for r in range(ROWS_N):
        for z in range(Z_N):
            for u in range(XH_N):
                for v in range(CORE_N):
                    src = ((r * Z_N + z) * XH_N + u) * CORE_N + v
                    dst = ((3 * (z - r) % Z_N * Z_N + z) * XH_N + v) * CORE_N + u
                    perm.append((src, dst))
    plane = lax.ppermute(plane, ALL, perm)
    pieces = [piece(plane, xh_at, 2 * rows), swap(piece(plane, 1 - xh_at, 2 * rows), "xh")]
    late_parts = lax.all_to_all(late_sum, "z", split_axis=0, concat_axis=0, tiled=True)
    part_there = swap(piece(part, 1 - xh_at, 2 * rows), "xh")
    late_parts, part_there, pieces, chip_chooser, chooser, table, send_grad = (
        lax.optimization_barrier(
            (late_parts, part_there, pieces, chip_chooser, chooser, table, send_grad)
        )
    )
    part_here = piece(part, xh_at, 2 * rows)
    bias = piece(cross_bias, core_at, half).reshape(1, half)
    first = (xh_at == 0).astype(jnp.int32).reshape(1)
    send = send_rows_of(
        first, *pieces, part_here, part_there, late_parts, bias, chip_chooser, send_grad
    )
    routed = lax.all_to_all(send, COL, split_axis=0, concat_axis=0, tiled=True)
    grad = routed[:, :, half:]
    routed_grad = jnp.concatenate([grad[:, :CAP], grad[:, CAP:]], axis=2).reshape(slots, share)
    routed = routed.reshape(COL_N // 2, 2, 2 * CAP, half + lanes)

    weight = expert_weight[0]
    pre = expert_call(forward_kernel, (ROWS_N, slots, share), routed, weight)
    parts = lax.all_to_all(pre, "row", split_axis=0, concat_axis=0, tiled=True)
    preact = jnp.sum(parts.astype(jnp.float32), axis=0)
    sigma = jax.nn.sigmoid(preact)
    activated = (preact * sigma).astype(jnp.bfloat16)
    slope = (
        routed_grad.astype(jnp.float32) * (sigma * (1.0 + preact * (1.0 - sigma)))
    ).astype(jnp.bfloat16)
    slopes = lax.all_to_all(
        jnp.broadcast_to(slope[None], (ROWS_N, slots, share)),
        "row",
        split_axis=0,
        concat_axis=0,
        tiled=True,
    )
    answer = expert_call(back_kernel, (slots, width + share), slopes, activated, weight)

    returned = lax.all_to_all(
        answer.reshape(COL_N, CAP, width + share), COL, split_axis=0, concat_axis=0, tiled=True
    ).reshape(slots, width + share)
    pull = (((0,), (0,)), ((), ()))
    pair_act = lax.dot_general(
        table, returned[:, width:], pull, preferred_element_type=jnp.float32
    )
    combined = jnp.sum(
        route_gates[:, :, None] * pair_act.reshape(rows, 2, share), axis=1
    ).astype(jnp.bfloat16)
    cross_grad = lax.dot_general(
        chooser, returned[:, :width], pull, preferred_element_type=jnp.float32
    ).astype(jnp.bfloat16)
    return combined, cross_grad


def solution(mesh):
    split = Mesh(mesh.devices.reshape(ROWS_N, Z_N, XH_N, CORE_N), ALL)
    return jax.shard_map(
        local,
        mesh=split,
        in_specs=(
            P(None, COL),
            P("row", COL),
            P("row"),
            P(COL, None),
            P(COL, None),
            P(COL, "row", None),
            P(COL, None),
        ),
        out_specs=(P(COL, "row"), P(COL, "row")),
        check_vma=False,
    )
```
